256 devices in a mesh: pole: 8 (over z), snode: 32 (over y, x, core).
Axes of the slice: x: 4, y: 4, z: 8, core: 2. Of those that a mesh axis runs over, the one named last changes fastest.
Arguments:
- pole_weight: float32 [8, 2], P('pole'), may hold values from -1 to 1
- root_factor: float32 [8, 2, 1024, 1024], P('pole', None, 'snode'), may hold values from -3 to 3, as said below
- leaf_factor: float32 [8, 64, 2, 512, 512], P('pole', 'snode'), may hold values from -3 to 3, as said below
- leaf_upper: float32 [8, 64, 2, 512, 512], P('pole', 'snode'), may hold values from -0.25 to 0.25
- leaf_lower: float32 [8, 64, 2, 512, 512], P('pole', 'snode'), may hold values from -0.25 to 0.25
- face_tiles: int32 [64, 2], P('snode'), may hold values from 0 to 3, all different within a row
Outputs:
- root_density: float32 [1024], P('snode')
- leaf_density: float32 [64, 512], P('snode')
- face_density: float32 [64, 512, 512], P('snode')
The draws below stay inside these ranges and needn't reach their ends.
Inputs may be any that keep to these rules, and one draw needn't show every extreme that they name: `face_tiles`: each row names 2 different root tiles; every root tile is named by some row. `root_factor`: diagonal tiles hold inverted pivot blocks, the other tiles the unit triangular factors' tiles. `leaf_factor`: laid out as root_factor, with 2 tiles.
All inputs are finite; a program needn't handle non-finite values.
Results may differ from the reference program's by a relative error of at most 0.0003.
Values sent between devices are 32-bit elements; how exact they have to be, the bound alone decides.
A program may use at most 128 MiB of HBM per device.

```python
import jax
import jax.numpy as jnp
from jax import lax

B = 256
NR = 4
NC = 2
FACES = 2
POLES = 8
SUPERS = 64
ROOT = 1024
LEAF = 512
FACE = 512


def with_pivots(key, noise, lead):
    size = noise.shape[-1]
    scale_key, phase_key = jax.random.split(key)
    scales = jnp.exp(jax.random.uniform(scale_key, lead + (size,), jnp.float32, jnp.log(0.5), jnp.log(2.0)))
    phases = jax.random.uniform(phase_key, lead + (size,), jnp.float32, -0.3, 0.3)
    positions = jnp.arange(size)
    identity = (positions[:, None] == positions[None, :]).astype(jnp.float32)
    real_part = noise[..., 0, :, :] + identity * scales[..., :, None]
    imag_part = noise[..., 1, :, :] + identity * phases[..., :, None]
    return jnp.stack([real_part, imag_part], axis=-3)


def draw_root_factor(key, part):
    key = jax.random.fold_in(key, 11)
    noise_key, pivot_key = jax.random.split(key)
    shape = (POLES, 2, ROOT, ROOT)
    noise = jax.random.truncated_normal(noise_key, -4.0, 4.0, shape, jnp.float32)
    return with_pivots(pivot_key, noise * (0.3 / B ** 0.5), (POLES,))


def draw_leaf_factor(key, part):
    key = jax.random.fold_in(key, 12)
    noise_key, pivot_key = jax.random.split(key)
    shape = (POLES, SUPERS, 2, LEAF, LEAF)
    noise = jax.random.truncated_normal(noise_key, -4.0, 4.0, shape, jnp.float32)
    return with_pivots(pivot_key, noise * (0.3 / B ** 0.5), (POLES, SUPERS))


def levels(stream_key, shape, cuts, smallest, top_value):
    factor_of, own = 1.0, jax.random.fold_in(stream_key, 6)
    for axis_at, parts in cuts:
        steps = jnp.exp(jax.random.uniform(jax.random.fold_in(own, axis_at), (parts,), jnp.float32, smallest / len(cuts), top_value / len(cuts)))
        factor_of = factor_of * jnp.repeat(steps, shape[axis_at] // parts).reshape([-1 if axis == axis_at else 1 for axis in range(len(shape))])
    return factor_of


def distinct(rng, rows, number_of, top, lift):
    ranking = jax.random.permutation(jax.random.fold_in(rng, 1), number_of)
    boost = ranking
    for power in range(3):
        boost = boost * boost // number_of
    boost = boost * lift // number_of
    lots = jax.random.randint(jax.random.fold_in(rng, 2), (rows, number_of), 0, 4096) + boost
    holders = jax.random.permutation(jax.random.fold_in(rng, 3), rows)[jnp.arange(number_of) % rows]
    lots = jnp.where(jnp.arange(rows)[:, None] == holders[None, :], 1 << 14, lots)
    merit = lots * number_of + jnp.arange(number_of)
    return lax.top_k(merit.astype(jnp.int32), top)[1].astype(jnp.int32)


def scatter_about(key, extent, deviation, bound, shards=(), held_as=jnp.bfloat16):
    drawn = jax.random.normal(key, extent, jnp.float32) * deviation
    if len(shards) > 0:
        drawn = levels(key, extent, shards, -0.22, 0.18) * drawn
    return jnp.clip(drawn, min=-bound, max=bound).astype(held_as)


def setup_inputs(seed: int = 0) -> dict:
    splits = jax.random.split(jax.random.key(seed), 7)
    pole_weight = jnp.clip(jax.random.uniform(splits[0], (POLES, 2), jnp.float32, -1.0, 1.0) * levels(splits[0], (POLES, 2), ((0, 8),), -0.4, 0.0), -1.0, 1.0)
    root_factor = draw_root_factor(jax.random.fold_in(splits[6], 71), 0)
    leaf_factor = draw_leaf_factor(jax.random.fold_in(splits[6], 71), 0)
    leaf_upper = scatter_about(splits[3], (POLES, SUPERS, 2, LEAF, FACE), FACE ** -0.5, 0.25, ((0, 8), (1, 32)), jnp.float32)
    leaf_lower = scatter_about(splits[4], (POLES, SUPERS, 2, FACE, LEAF), FACE ** -0.5, 0.25, ((0, 8), (1, 32)), jnp.float32)
    face_tiles = distinct(splits[5], SUPERS, NR, FACES, 0)
    return {"pole_weight": pole_weight, "root_factor": root_factor, "leaf_factor": leaf_factor, "leaf_upper": leaf_upper, "leaf_lower": leaf_lower, "face_tiles": face_tiles}


def complex_dot(first, second):
    highest = lax.Precision.HIGHEST
    real_part = jnp.dot(first[0], second[0], precision=highest, preferred_element_type=jnp.float32) - jnp.dot(first[1], second[1], precision=highest, preferred_element_type=jnp.float32)
    imag_part = jnp.dot(first[0], second[1], precision=highest, preferred_element_type=jnp.float32) + jnp.dot(first[1], second[0], precision=highest, preferred_element_type=jnp.float32)
    return jnp.stack([real_part, imag_part])


def selected_inverse(factor, blocks):
    last_begin = (blocks - 1) * B
    inverse = factor[:, last_begin:, last_begin:]
    for number in range(blocks - 2, -1, -1):
        row_begin = number * B
        finish = row_begin + B
        upper_part = factor[:, row_begin:finish, finish:]
        lower_part = factor[:, finish:, row_begin:finish]
        row_block = -complex_dot(upper_part, inverse)
        column_block = -complex_dot(inverse, lower_part)
        corner = factor[:, row_begin:finish, row_begin:finish] - complex_dot(upper_part, column_block)
        top_rows = jnp.concatenate([corner, row_block], axis=2)
        bottom_rows = jnp.concatenate([column_block, inverse], axis=2)
        inverse = jnp.concatenate([top_rows, bottom_rows], axis=1)
    return inverse


def face_rows(face_list):
    offsets = jnp.arange(B, dtype=jnp.int32)
    return (face_list.astype(jnp.int32)[:, None] * B + offsets[None, :]).reshape(-1)


def reference(pole_weight, root_factor, leaf_factor, leaf_upper, leaf_lower, face_tiles):
    root_density = jnp.zeros((ROOT,), jnp.float32)
    leaf_density = jnp.zeros((SUPERS, LEAF), jnp.float32)
    face_density = jnp.zeros((SUPERS, FACE, LEAF), jnp.float32)
    for pole_number in range(POLES):
        real_weight = pole_weight[pole_number, 0]
        imag_weight = pole_weight[pole_number, 1]
        root_inverse = selected_inverse(root_factor[pole_number], NR)
        root_diagonal = jnp.diagonal(root_inverse, axis1=1, axis2=2)
        root_density = root_density + real_weight * root_diagonal[0] - imag_weight * root_diagonal[1]

        def one_leaf(items):
            factor, upper_side, lower_side, face_list = items
            leaf_inverse = selected_inverse(factor, NC)
            picked = face_rows(face_list)
            coupled = jnp.take(jnp.take(root_inverse, picked, axis=1), picked, axis=2)
            column_block = -complex_dot(coupled, lower_side)
            diagonal_block = leaf_inverse - complex_dot(upper_side, column_block)
            return jnp.diagonal(diagonal_block, axis1=1, axis2=2), column_block

        diagonals, columns = lax.map(one_leaf, (leaf_factor[pole_number], leaf_upper[pole_number], leaf_lower[pole_number], face_tiles))
        leaf_density = leaf_density + real_weight * diagonals[:, 0] - imag_weight * diagonals[:, 1]
        face_density = face_density + real_weight * columns[:, 0] - imag_weight * columns[:, 1]
    return root_density, leaf_density, face_density
```

```python
import functools

import jax
import jax.numpy as jnp
from jax import lax
from jax.experimental import pallas as pl
from jax.experimental.pallas import tpu as pltpu
from jax.sharding import PartitionSpec as P

NR = 4
X = 4
Y = 4
Z = 8
F32 = jnp.float32
BF16 = jnp.bfloat16


def split(value):
    high = value.astype(BF16)
    return high, (value - high.astype(F32)).astype(BF16)


def as_left(rh, rl, ih, il):
    high = jnp.concatenate([jnp.concatenate([rh, -ih], 1), jnp.concatenate([ih, rh], 1)], 0)
    low = jnp.concatenate([jnp.concatenate([rl, -il], 1), jnp.concatenate([il, rl], 1)], 0)
    return jnp.concatenate([high, high, low], 1)


def as_right(rh, rl, ih, il):
    return jnp.concatenate([rh, ih, rl, il, rh, ih], 0)


def product(left, right):
    return jnp.dot(left, right, preferred_element_type=F32)


def fold_rows(value):
    rows, cols = value.shape
    return jnp.sum(value.reshape(rows // 8, 8, cols), axis=0)


def kernel(
    T,
    w_ref, faces_ref, root_hbm, lf_hbm, lu_hbm, ll_hbm,
    face_out, leaf_out, root_out,
    root_all, fh, fl, gh, gl, lf, lu, lut, ll, lh, lo, contrib, rs_buf, leaf_acc, small,
    in_sem, p1_s, p1_r, p2_s, p2_r, sib_s, sib_r, rs_s, rs_r, ag_s, ag_r, sm_s, sm_r,
):
    z = lax.axis_index("pole")
    s = lax.axis_index("snode")
    core = s % 2
    x = (s // 2) % X
    y = s // (2 * X)
    band = root_hbm.shape[1]
    half = band // 2
    sub = T // 4

    def at_xy(yy, xx, cc):
        return {"snode": (yy * X + xx) * 2 + cc}

    xp, xm, x2 = (x + 1) % X, (x + X - 1) % X, (x + 2) % X
    yp, ym, y2 = (y + 1) % Y, (y + Y - 1) % Y, (y + 2) % Y
    zp, zm = (z + 1) % Z, (z + Z - 1) % Z
    east, west = at_xy(y, xp, core), at_xy(y, xm, core)
    north, south = at_xy(yp, x, core), at_xy(ym, x, core)
    mate = at_xy(y, x, 1 - core)
    above, below = {"pole": zp}, {"pole": zm}

    def remote(src, dst, send, recv, to):
        return pltpu.make_async_remote_copy(
            src_ref=src, dst_ref=dst, send_sem=send, recv_sem=recv,
            device_id=to, device_id_type=pl.DeviceIdType.MESH,
        )

    sent = []

    def push(src, dst, send, recv, to):
        copy = remote(src, dst, send, recv, to)
        copy.start()
        sent.append(copy)

    def arrived(dst, send, recv, to):
        remote(dst, dst, send, recv, to).wait_recv()

    barrier = pltpu.get_barrier_semaphore()
    for to in (east, west, north, south, mate, above, below):
        pl.semaphore_signal(barrier, inc=1, device_id=to, device_id_type=pl.DeviceIdType.MESH)

    loads = [
        pltpu.make_async_copy(root_hbm, root_all.at[:, y, x, core], in_sem.at[0]),
        pltpu.make_async_copy(lf_hbm, lf, in_sem.at[1]),
        pltpu.make_async_copy(lu_hbm, lu, in_sem.at[2]),
        pltpu.make_async_copy(ll_hbm, ll, in_sem.at[3]),
    ]
    loads[0].start()
    pl.semaphore_wait(barrier, 7)

    for part, plus, minus in ((0, east, west), (1, north, south)):
        for number, to in ((0, plus), (1, minus)):
            push(root_hbm.at[part], root_all.at[part, y, x, core],
                 p1_s.at[part, number], p1_r.at[part, number], to)
    for load in loads[1:]:
        load.start()
    for part, plus, minus, near in (
        (0, east, west, (root_all.at[0, y, xm, core], root_all.at[0, y, xp, core])),
        (1, north, south, (root_all.at[1, ym, x, core], root_all.at[1, yp, x, core])),
    ):
        arrived(near[0], p1_s.at[part, 0], p1_r.at[part, 0], plus)
        ahead = near[0].at[pl.ds(0, half)]
        push(ahead, ahead, p1_s.at[part, 2], p1_r.at[part, 2], plus)
        arrived(near[1], p1_s.at[part, 1], p1_r.at[part, 1], minus)
        back = near[1].at[pl.ds(half, half)]
        push(back, back, p1_s.at[part, 3], p1_r.at[part, 3], minus)
    loads[0].wait()
    for part, plus, minus, far in (
        (0, east, west, root_all.at[0, y, x2, core]),
        (1, north, south, root_all.at[1, y2, x, core]),
    ):
        arrived(far.at[pl.ds(0, half)], p1_s.at[part, 2], p1_r.at[part, 2], plus)
        arrived(far.at[pl.ds(half, half)], p1_s.at[part, 3], p1_r.at[part, 3], minus)

    def lines(wave, other):
        cols = pl.ds(wave * T, T)
        real = lambda yy, xs=slice(None): root_all.at[0, yy, xs, other, :, cols]
        imag = lambda xx, ys=slice(None): root_all.at[1, ys, xx, other, :, cols]
        return real, imag

    low, up = pl.ds(0, 2), pl.ds(2, 2)

    def send_near(wave):
        real, imag = lines(wave, core)
        for number, piece, to in (
            (0, real(y), north), (1, real(y), south), (4, imag(x), east), (5, imag(x), west)
        ):
            push(piece, piece, p2_s.at[wave, number], p2_r.at[wave, number], to)

    def to_mate(wave, number, piece):
        push(piece, piece, sib_s.at[wave, number], sib_r.at[wave, number], mate)

    def relay_near(wave):
        real, imag = lines(wave, core)
        for number, piece, ahead, to in (
            (0, real(ym), real(ym, low), north), (1, real(yp), real(yp, up), south),
            (4, imag(xm), imag(xm, low), east), (5, imag(xp), imag(xp, up), west),
        ):
            arrived(piece, p2_s.at[wave, number], p2_r.at[wave, number], to)
            push(ahead, ahead, p2_s.at[wave, number + 2], p2_r.at[wave, number + 2], to)
        to_mate(wave, 0, real(ym))
        to_mate(wave, 1, real(yp))
        to_mate(wave, 2, imag(xm))
        to_mate(wave, 3, imag(xp))

    def relay_far(wave):
        real, imag = lines(wave, core)
        for number, piece, to in (
            (2, real(y2, low), north), (3, real(y2, up), south),
            (6, imag(x2, low), east), (7, imag(x2, up), west),
        ):
            arrived(piece, p2_s.at[wave, number], p2_r.at[wave, number], to)
        to_mate(wave, 4, real(y2))
        to_mate(wave, 5, imag(x2))

    def from_mate(wave):
        real, imag = lines(wave, 1 - core)
        for number, piece in enumerate(
            (real(ym), real(yp), imag(xm), imag(xp), real(y2), imag(x2))
        ):
            arrived(piece, sib_s.at[wave, number], sib_r.at[wave, number], mate)

    send_near(3)
    send_near(2)
    own_line = (root_all.at[0, y, :, core], root_all.at[1, :, x, core])
    for part in range(2):
        push(own_line[part], own_line[part], sib_s.at[NR, part], sib_r.at[NR, part], mate)

    wr = w_ref[0, 0]
    wi = w_ref[0, 1]
    eye = (
        lax.broadcasted_iota(jnp.int32, (T, T), 0) == lax.broadcasted_iota(jnp.int32, (T, T), 1)
    ).astype(F32)

    def weighted_diagonal(real, imag):
        return jnp.sum(fold_rows((wr * real - wi * imag) * eye), axis=0, keepdims=True)

    first, second = pl.ds(0, T), pl.ds(T, T)

    def leaf_inverse(leaf):
        pr, pi = lf[leaf, 0, second, second], lf[leaf, 1, second, second]
        inner = product(
            as_left(*split(pr), *split(pi)),
            as_right(*split(lf[leaf, 0, second, first]), *split(lf[leaf, 1, second, first])),
        )
        ur, ui = lf[leaf, 0, first, second].T, lf[leaf, 1, first, second].T
        tr, ti = inner[:T], inner[T:]
        total = ur * (wr * tr - wi * ti) - ui * (wr * ti + wi * tr)
        base = weighted_diagonal(lf[leaf, 0, first, first], lf[leaf, 1, first, first])
        rows = lax.broadcasted_iota(jnp.int32, (8, T), 0) == 0
        leaf_acc[leaf, 0] = fold_rows(total) + jnp.where(rows, base, 0.0)
        leaf_acc[leaf, 1] = jnp.where(rows, weighted_diagonal(pr, pi), 0.0)

    def turn_upper(leaf):
        for part in range(2):
            for row in (first, second):
                for col in (first, second):
                    lut[leaf, part, col, row] = lu[leaf, part, row, col].T

    def split_lower(leaf):
        for part in range(2):
            for row in (first, second):
                lh[leaf, part, row], lo[leaf, part, row] = split(ll[leaf, part, row])

    def leaf_loop(body):
        def step(leaf, carry):
            body(leaf)
            return carry
        lax.fori_loop(0, 2, step, 0)

    loads[1].wait()
    leaf_loop(leaf_inverse)

    def load_wave(wave):
        for part in range(2):
            def step(row, carry):
                tile = root_all[part, row, :, :, :, pl.ds(wave * T, T)].reshape(T, T)
                fh[part, row, wave], fl[part, row, wave] = split(tile)
                return carry
            lax.fori_loop(0, NR, step, 0)

    def tile_of(high, lower, row, col):
        return high[0, row, col], lower[0, row, col], high[1, row, col], lower[1, row, col]

    def chain(lefts, rights):
        left = jnp.concatenate([as_left(*item) for item in lefts], 1)
        right = jnp.concatenate([as_right(*item) for item in rights], 0)
        return product(left, right)

    def put(row, col, value):
        gh[0, row, col], gl[0, row, col] = split(value[:T])
        gh[1, row, col], gl[1, row, col] = split(value[T:])

    def upper(k, col):
        after = range(k + 1, NR)
        put(k, col, -chain([tile_of(fh, fl, k, m) for m in after], [tile_of(gh, gl, m, col) for m in after]))

    def lower(row, k):
        after = range(k + 1, NR)
        put(row, k, -chain([tile_of(gh, gl, row, m) for m in after], [tile_of(fh, fl, m, k) for m in after]))

    def pivot(k):
        cols = pl.ds(k * T, T)
        real = root_all[0, k, :, :, :, cols].reshape(T, T)
        imag = root_all[1, k, :, :, :, cols].reshape(T, T)
        after = range(k + 1, NR)
        if after:
            taken = chain([tile_of(fh, fl, k, m) for m in after], [tile_of(gh, gl, m, k) for m in after])
            real = real - taken[:T]
            imag = imag - taken[T:]
        gh[0, k, k], gl[0, k, k] = split(real)
        gh[1, k, k], gl[1, k, k] = split(imag)
        small[z, 4 + k : 5 + k] = weighted_diagonal(real, imag)

    relay_near(3)
    send_near(1)
    loads[3].wait()
    leaf_loop(split_lower)
    relay_far(3)
    loads[2].wait()
    leaf_loop(turn_upper)
    relay_near(2)
    send_near(0)
    for part in range(2):
        theirs = (root_all.at[0, y, :, 1 - core], root_all.at[1, :, x, 1 - core])[part]
        arrived(theirs, sib_s.at[NR, part], sib_r.at[NR, part], mate)
    from_mate(3)
    load_wave(3)
    pivot(3)
    upper(2, 3)
    relay_far(2)
    from_mate(2)
    relay_near(1)
    load_wave(2)
    lower(3, 2)
    pivot(2)
    upper(1, 3)
    upper(1, 2)
    relay_far(1)
    relay_near(0)
    from_mate(1)
    load_wave(1)
    lower(3, 1)
    lower(2, 1)
    pivot(1)
    relay_far(0)
    upper(0, 3)
    upper(0, 2)
    upper(0, 1)
    from_mate(0)
    load_wave(0)
    lower(3, 0)
    lower(2, 0)
    lower(1, 0)
    pivot(0)

    def quarter(leaf, number):
        qr, qc = number // 2, number % 2
        cols = pl.ds(pl.multiple_of(qc * T, T), T)
        row = faces_ref[leaf, qr]
        lefts, rights = [], []
        for face in range(2):
            col = faces_ref[leaf, face]
            lefts.append(tile_of(gh, gl, row, col))
            inner = pl.ds(face * T, T)
            rights.append((lh[leaf, 0, inner, cols], lo[leaf, 0, inner, cols],
                           lh[leaf, 1, inner, cols], lo[leaf, 1, inner, cols]))
        block = -chain(lefts, rights)
        real, imag = block[:T], block[T:]
        dr = wr * real - wi * imag
        di = wr * imag + wi * real
        contrib[leaf, number] = dr.reshape(2, 2, sub, T)
        rows = pl.ds(pl.multiple_of(qr * T, T), T)
        taken = lut[leaf, 0, rows, cols] * dr - lut[leaf, 1, rows, cols] * di
        leaf_acc[leaf, qc] = leaf_acc[leaf, qc] - fold_rows(taken)

    def quarters(step):
        def body(leaf, carry):
            number = (z // 2 + (2 * leaf - 1) * step + 8) % 4
            quarter(leaf, number)
            return carry
        lax.fori_loop(0, 2, body, 0)

    def chunk(way, step):
        return (z - step + 16) % Z if way == 0 else (z + step) % Z

    onward = (above, below)

    def mine(way, step, piece):
        number = chunk(way, step)
        return contrib.at[way, number // 2, number % 2, piece]

    def place(way, step, piece):
        number = chunk(way, step)
        block, part = number // 2, number % 2
        row = pl.multiple_of((block // 2) * T + part * (2 * sub) + piece * sub, sub)
        col = pl.multiple_of((block % 2) * T, T)
        return face_out.at[way, pl.ds(row, sub), pl.ds(col, T)]

    def scatter_send(way, step, piece):
        src = mine(way, 0, piece) if step == 0 else rs_buf.at[way, step - 1, piece]
        push(src, rs_buf.at[way, step, piece], rs_s.at[way, step, piece],
             rs_r.at[way, step, piece], onward[way])

    def gather_send(way, step, piece):
        where = place(way, 7 + step, piece)
        push(where, where, ag_s.at[way, step, piece], ag_r.at[way, step, piece], onward[way])

    ways = [(way, piece) for piece in range(2) for way in range(2)]
    quarters(0)
    for way, piece in ways:
        scatter_send(way, 0, piece)
    quarters(1)
    for step in range(Z - 1):
        for way, piece in ways:
            slot = rs_buf.at[way, step, piece]
            arrived(slot, rs_s.at[way, step, piece], rs_r.at[way, step, piece], onward[way])
            if step < Z - 2:
                slot[...] = slot[...] + mine(way, step + 1, piece)[...]
                scatter_send(way, step + 1, piece)
            else:
                place(way, step + 1, piece)[...] = slot[...] + mine(way, step + 1, piece)[...]
                gather_send(way, 0, piece)
        if step < 2:
            quarters(step + 2)
    for leaf in range(2):
        for col in range(2):
            row = 2 * leaf + col
            small[z, row : row + 1] = jnp.sum(leaf_acc[leaf, col], axis=0, keepdims=True)

    def small_send(step):
        where = small.at[(z - step + Z) % Z]
        push(where, where, sm_s.at[step], sm_r.at[step], above)

    small_send(0)
    for step in range(Z - 1):
        arrived(small.at[(z - step - 1 + Z) % Z], sm_s.at[step], sm_r.at[step], above)
        if step < Z - 2:
            small_send(step + 1)
        for way, piece in ways:
            arrived(place(way, 8 + step, piece), ag_s.at[way, step, piece],
                    ag_r.at[way, step, piece], onward[way])
            if step < Z - 2:
                gather_send(way, step + 1, piece)
    total = jnp.sum(small[...], axis=0)
    for leaf in range(2):
        for col in range(2):
            row = 2 * leaf + col
            leaf_out[leaf : leaf + 1, col * T : (col + 1) * T] = total[row : row + 1]
    root_row = jnp.zeros((1, T), F32)
    for k in range(NR):
        root_row = root_row + jnp.where(y == k, total[4 + k : 5 + k], 0.0)
    root_row = pltpu.roll(root_row, (T - (x * 2 + core) * band) % T, 1)
    root_out[...] = root_row[:, :128]
    for copy in sent:
        copy.wait_send()


def per_device(pole_weight, root_factor, leaf_factor, leaf_upper, leaf_lower, face_tiles):
    T = root_factor.shape[-1] // NR
    band = root_factor.shape[2]
    wide = 2 * T
    whole = pl.BlockSpec(memory_space=pl.ANY)
    scalars = pl.BlockSpec(memory_space=pltpu.SMEM)
    vmem = pl.BlockSpec(memory_space=pltpu.VMEM)
    dma = pltpu.SemaphoreType.DMA
    face, leaf, root = pl.pallas_call(
        functools.partial(kernel, T),
        out_shape=(
            jax.ShapeDtypeStruct((2, wide, wide), F32),
            jax.ShapeDtypeStruct((2, wide), F32),
            jax.ShapeDtypeStruct((1, 128), F32),
        ),
        in_specs=[scalars, scalars, whole, whole, whole, whole],
        out_specs=(vmem, vmem, vmem),
        scratch_shapes=[
            pltpu.VMEM((2, Y, X, 2, band, NR * T), F32),
            pltpu.VMEM((2, NR, NR, T, T), BF16),
            pltpu.VMEM((2, NR, NR, T, T), BF16),
            pltpu.VMEM((2, NR, NR, T, T), BF16),
            pltpu.VMEM((2, NR, NR, T, T), BF16),
            pltpu.VMEM((2, 2, wide, wide), F32),
            pltpu.VMEM((2, 2, wide, wide), F32),
            pltpu.VMEM((2, 2, wide, wide), F32),
            pltpu.VMEM((2, 2, wide, wide), F32),
            pltpu.VMEM((2, 2, wide, wide), BF16),
            pltpu.VMEM((2, 2, wide, wide), BF16),
            pltpu.VMEM((2, 4, 2, 2, T // 4, T), F32),
            pltpu.VMEM((2, Z - 1, 2, T // 4, T), F32),
            pltpu.VMEM((2, 2, 8, T), F32),
            pltpu.VMEM((Z, 8, T), F32),
            dma((4,)),
            dma((2, 4)), dma((2, 4)),
            dma((NR, 8)), dma((NR, 8)),
            dma((NR + 1, 6)), dma((NR + 1, 6)),
            dma((2, Z - 1, 2)), dma((2, Z - 1, 2)),
            dma((2, Z - 1, 2)), dma((2, Z - 1, 2)),
            dma((Z - 1,)), dma((Z - 1,)),
        ],
        compiler_params=pltpu.CompilerParams(
            collective_id=0, has_side_effects=True, vmem_limit_bytes=60 * 1024 * 1024
        ),
    )(pole_weight, face_tiles, root_factor[0], leaf_factor[0], leaf_upper[0], leaf_lower[0])
    return root[0, :band], leaf, face


def solution(mesh):
    return jax.shard_map(
        per_device,
        mesh=mesh,
        in_specs=(
            P("pole", None),
            P("pole", None, "snode", None),
            P("pole", "snode", None, None, None),
            P("pole", "snode", None, None, None),
            P("pole", "snode", None, None, None),
            P("snode", None),
        ),
        out_specs=(P("snode"), P("snode", None), P("snode", None, None)),
        check_vma=False,
    )
```

```python
import functools

import jax
import jax.numpy as jnp
from jax import lax
from jax.experimental import pallas as pl
from jax.experimental.pallas import tpu as pltpu
from jax.sharding import PartitionSpec as P

NR = 4
X = 4
Y = 4
Z = 8
HOPS = Z // 2
PIECES = 2
F32 = jnp.float32
BF16 = jnp.bfloat16


def split(value):
    high = value.astype(BF16)
    return high, (value - high.astype(F32)).astype(BF16)


def product(left, right):
    def three(a, b):
        ah, al = (jnp.concatenate([item[n] for item in left], 1) for n in (a, a + 1))
        bh, bl = (jnp.concatenate([item[n] for item in right], 0) for n in (b, b + 1))
        return jnp.dot(
            jnp.concatenate([ah, ah, al], 1), jnp.concatenate([bh, bl, bh], 0), preferred_element_type=F32
        )

    return jnp.concatenate([three(0, 0) - three(2, 2), three(0, 2) + three(2, 0)], 0)


def fold_rows(value):
    rows, cols = value.shape
    return jnp.sum(value.reshape(rows // 8, 8, cols), axis=0)


def kernel(
    T,
    w_ref, faces_ref, root_hbm, lf_hbm, lu_hbm, ll_hbm,
    face_out, leaf_out, root_out,
    root_all, fh, fl, gh, gl, lf, lu, lut, ll, lh, lo, pivots, contrib, rs_buf, leaf_acc, small,
    in_sem, p1_s, p1_r, p2_s, p2_r, sib_s, sib_r, rs_s, rs_r, ag_s, ag_r, sm_s, sm_r,
):
    z = lax.axis_index("pole")
    s = lax.axis_index("snode")
    core = s % 2
    x = (s // 2) % X
    y = s // (2 * X)
    band = root_hbm.shape[1]
    half = band // 2
    sub = T // 2 // PIECES

    def at_xy(yy, xx, cc):
        return {"snode": (yy * X + xx) * 2 + cc}

    xp, xm, x2 = (x + 1) % X, (x + X - 1) % X, (x + 2) % X
    yp, ym, y2 = (y + 1) % Y, (y + Y - 1) % Y, (y + 2) % Y
    zp, zm = (z + 1) % Z, (z + Z - 1) % Z
    east, west = at_xy(y, xp, core), at_xy(y, xm, core)
    north, south = at_xy(yp, x, core), at_xy(ym, x, core)
    mate = at_xy(y, x, 1 - core)
    above, below = {"pole": zp}, {"pole": zm}

    def remote(src, dst, send, recv, to):
        return pltpu.make_async_remote_copy(
            src_ref=src, dst_ref=dst, send_sem=send, recv_sem=recv,
            device_id=to, device_id_type=pl.DeviceIdType.MESH,
        )

    sent = []

    def push(src, dst, send, recv, to):
        copy = remote(src, dst, send, recv, to)
        copy.start()
        sent.append(copy)

    def arrived(dst, send, recv, to):
        remote(dst, dst, send, recv, to).wait_recv()

    barrier = pltpu.get_barrier_semaphore()
    for to in (east, west, north, south, mate, above, below):
        pl.semaphore_signal(barrier, inc=1, device_id=to, device_id_type=pl.DeviceIdType.MESH)

    loads = [
        pltpu.make_async_copy(root_hbm, root_all.at[:, y, x, core], in_sem.at[0]),
        pltpu.make_async_copy(lf_hbm, lf, in_sem.at[1]),
        pltpu.make_async_copy(lu_hbm, lu, in_sem.at[2]),
        pltpu.make_async_copy(ll_hbm, ll, in_sem.at[3]),
    ]
    loads[0].start()
    pl.semaphore_wait(barrier, 7)

    everything = slice(None)
    fore, rear = pl.ds(0, half), pl.ds(half, half)
    halves = (pl.ds(2 * T, 2 * T), pl.ds(0, 2 * T))
    tiles = [pl.ds(wave * T, T) for wave in range(NR)]
    along = ((y, ym, yp, y2), (x, xm, xp, x2))
    across = ((x, xm, xp, x2), (y, ym, yp, y2))
    first_ways = ((east, west), (north, south))
    second_ways = ((north, south), (east, west))

    def spot(part, line, cross, rows, cols, other=core):
        if part == 0:
            return root_all.at[0, line, cross, other, rows, cols]
        return root_all.at[1, cross, line, other, rows, cols]

    def line_send(part, h):
        for number, to in enumerate(first_ways[part]):
            push(root_hbm.at[part, :, halves[h]], spot(part, along[part][0], across[part][0], everything, halves[h]),
                 p1_s.at[part, h, number], p1_r.at[part, h, number], to)

    def line_near(part, h):
        for number, to in enumerate(first_ways[part]):
            cross = across[part][1 + number]
            arrived(spot(part, along[part][0], cross, everything, halves[h]),
                    p1_s.at[part, h, number], p1_r.at[part, h, number], to)
            piece = spot(part, along[part][0], cross, (fore, rear)[number], halves[h])
            push(piece, piece, p1_s.at[part, h, 2 + number], p1_r.at[part, h, 2 + number], to)

    def line_far(part, h):
        for number, to in enumerate(first_ways[part]):
            arrived(spot(part, along[part][0], across[part][3], (fore, rear)[number], halves[h]),
                    p1_s.at[part, h, 2 + number], p1_r.at[part, h, 2 + number], to)

    def near_send(part, group, cut):
        cols = (halves if group == 0 else tiles)[cut]
        for number, to in enumerate(second_ways[part]):
            piece = spot(part, along[part][0], across[part][group], everything, cols)
            src = root_hbm.at[part, :, cols] if group == 0 else piece
            push(src, piece, p2_s.at[part, group, cut, number], p2_r.at[part, group, cut, number], to)

    def far_rows(group, number):
        if group in (0, 3):
            return (fore, rear)[number]
        return everything if group == 1 + number else None

    def near_in(part, group, cut):
        cols = (halves if group == 0 else tiles)[cut]
        for number, to in enumerate(second_ways[part]):
            line = along[part][1 + number]
            arrived(spot(part, line, across[part][group], everything, cols),
                    p2_s.at[part, group, cut, number], p2_r.at[part, group, cut, number], to)
            rows = far_rows(group, number)
            if rows is not None:
                piece = spot(part, line, across[part][group], rows, cols)
                push(piece, piece, p2_s.at[part, group, cut, 2 + number],
                     p2_r.at[part, group, cut, 2 + number], to)

    def far_in(part, group, cut):
        cols = (halves if group == 0 else tiles)[cut]
        for number, to in enumerate(second_ways[part]):
            rows = far_rows(group, number)
            if rows is not None:
                arrived(spot(part, along[part][3], across[part][group], rows, cols),
                        p2_s.at[part, group, cut, 2 + number], p2_r.at[part, group, cut, 2 + number], to)

    parts = (0, 1)

    def mate_lines(cut, numbers, cols, other):
        for part in parts:
            for number in numbers:
                yield part, number, spot(part, along[part][number], everything, everything, cols, other)

    def to_mate(cut, numbers, cols):
        for part, number, piece in mate_lines(cut, numbers, cols, core):
            push(piece, piece, sib_s.at[part, number, cut], sib_r.at[part, number, cut], mate)

    def from_mate(cut, numbers, cols):
        for part, number, piece in mate_lines(cut, numbers, cols, 1 - core):
            arrived(piece, sib_s.at[part, number, cut], sib_r.at[part, number, cut], mate)

    def relay_near(wave):
        for group in (1, 2, 3):
            for part in parts:
                near_in(part, group, wave)
        to_mate(wave, (1, 2), tiles[wave])

    def relay_far(wave):
        for group in (1, 2, 3):
            for part in parts:
                far_in(part, group, wave)
        to_mate(wave, (3,), tiles[wave])

    def waves_send(wave, groups):
        for group in groups:
            for part in parts:
                near_send(part, group, wave)

    def own_part(action, h):
        for part in parts:
            action(part, 0, h)

    def line_part(action, h):
        for part in parts:
            action(part, h)

    def own_line(h):
        to_mate(h, (0,), halves[h])

    def mate_line(h):
        from_mate(h, (0,), halves[h])

    line_part(line_send, 0)
    own_part(near_send, 0)
    for load in loads[1:]:
        load.start()

    wr = w_ref[0, 0]
    wi = w_ref[0, 1]
    eye = (
        lax.broadcasted_iota(jnp.int32, (T, T), 0) == lax.broadcasted_iota(jnp.int32, (T, T), 1)
    ).astype(F32)

    def weighted_diagonal(real, imag):
        return jnp.sum(fold_rows((wr * real - wi * imag) * eye), axis=0, keepdims=True)

    first, second = pl.ds(0, T), pl.ds(T, T)

    def leaf_inverse(leaf):
        pr, pi = lf[leaf, 0, second, second], lf[leaf, 1, second, second]
        inner = product(
            [split(pr) + split(pi)],
            [split(lf[leaf, 0, second, first]) + split(lf[leaf, 1, second, first])],
        )
        ur, ui = lf[leaf, 0, first, second].T, lf[leaf, 1, first, second].T
        tr, ti = inner[:T], inner[T:]
        total = ur * (wr * tr - wi * ti) - ui * (wr * ti + wi * tr)
        base = weighted_diagonal(lf[leaf, 0, first, first], lf[leaf, 1, first, first])
        rows = lax.broadcasted_iota(jnp.int32, (8, T), 0) == 0
        leaf_acc[leaf, 0] = fold_rows(total) + jnp.where(rows, base, 0.0)
        leaf_acc[leaf, 1] = jnp.where(rows, weighted_diagonal(pr, pi), 0.0)

    def turn_upper(leaf):
        for part in range(2):
            for row in (first, second):
                for col in (first, second):
                    lut[leaf, part, col, row] = lu[leaf, part, row, col].T

    def split_lower(leaf):
        for part in range(2):
            for row in (first, second):
                lh[leaf, part, row], lo[leaf, part, row] = split(ll[leaf, part, row])

    def load_wave(wave):
        for part in range(2):
            for row in range(NR):
                if row != wave:
                    tile = root_all[part, row, :, :, :, pl.ds(wave * T, T)].reshape(T, T)
                    fh[part, row, wave], fl[part, row, wave] = split(tile)

    def tile_of(high, lower, row, col):
        return high[0, row, col], lower[0, row, col], high[1, row, col], lower[1, row, col]

    def put(row, col, value):
        gh[0, row, col], gl[0, row, col] = split(value[:T])
        gh[1, row, col], gl[1, row, col] = split(value[T:])

    def uppers(k, cols):
        after = range(k + 1, NR)
        for col in cols:
            put(k, col, -product([tile_of(fh, fl, k, m) for m in after], [tile_of(gh, gl, m, col) for m in after]))

    def lowers(rows, k):
        after = range(k + 1, NR)
        for row in rows:
            put(row, k, -product([tile_of(gh, gl, row, m) for m in after], [tile_of(fh, fl, m, k) for m in after]))

    def pivot(k):
        cols = pl.ds(k * T, T)
        real = root_all[0, k, :, :, :, cols].reshape(T, T)
        imag = root_all[1, k, :, :, :, cols].reshape(T, T)
        after = range(k + 1, NR)
        if after:
            taken = product([tile_of(fh, fl, k, m) for m in after], [tile_of(gh, gl, m, k) for m in after])
            real = real - taken[:T]
            imag = imag - taken[T:]
        gh[0, k, k], gl[0, k, k] = split(real)
        gh[1, k, k], gl[1, k, k] = split(imag)
        pivots[k, 0] = real
        pivots[k, 1] = imag

    def root_diagonal(k):
        small[z, 4 + k : 5 + k] = weighted_diagonal(pivots[k, 0], pivots[k, 1])

    loads[1].wait()
    leaf_inverse(0)
    line_part(line_near, 0)
    waves_send(3, (1, 2))
    line_part(line_send, 1)
    waves_send(2, (1, 2))
    leaf_inverse(1)
    line_part(line_far, 0)
    waves_send(3, (3,))
    waves_send(2, (3,))
    loads[0].wait()
    own_line(0)
    own_part(near_send, 1)
    own_part(near_in, 0)
    line_part(line_near, 1)
    loads[3].wait()
    split_lower(0)
    relay_near(3)
    split_lower(1)
    line_part(line_far, 1)
    own_line(1)
    waves_send(1, (1, 2, 3))
    loads[2].wait()
    turn_upper(0)
    relay_near(2)
    own_part(far_in, 0)
    relay_far(3)
    own_part(near_in, 1)
    waves_send(0, (1, 2, 3))
    turn_upper(1)
    mate_line(0)
    from_mate(3, (1, 2, 3), tiles[3])
    load_wave(3)
    pivot(3)
    uppers(2, (3,))
    relay_near(1)
    relay_far(2)
    from_mate(2, (1, 2, 3), tiles[2])
    load_wave(2)
    lowers((3,), 2)
    pivot(2)
    relay_near(0)
    own_part(far_in, 1)
    relay_far(1)
    uppers(1, (3, 2))
    mate_line(1)
    from_mate(1, (1, 2, 3), tiles[1])
    load_wave(1)
    lowers((3, 2), 1)
    relay_far(0)
    pivot(1)
    uppers(0, (3, 2, 1))
    from_mate(0, (1, 2, 3), tiles[0])
    load_wave(0)
    lowers((3, 2, 1), 0)
    pivot(0)

    def quarter(leaf, number):
        qr, qc = number // 2, number % 2
        cols = pl.ds(pl.multiple_of(qc * T, T), T)
        row = faces_ref[leaf, qr]
        lefts, rights = [], []
        for face in range(2):
            col = faces_ref[leaf, face]
            lefts.append(tile_of(gh, gl, row, col))
            inner = pl.ds(face * T, T)
            rights.append((lh[leaf, 0, inner, cols], lo[leaf, 0, inner, cols],
                           lh[leaf, 1, inner, cols], lo[leaf, 1, inner, cols]))
        block = -product(lefts, rights)
        real, imag = block[:T], block[T:]
        dr = wr * real - wi * imag
        di = wr * imag + wi * real
        contrib[leaf, number] = dr.reshape(2, PIECES, sub, T)
        rows = pl.ds(pl.multiple_of(qr * T, T), T)
        taken = lut[leaf, 0, rows, cols] * dr - lut[leaf, 1, rows, cols] * di
        leaf_acc[leaf, qc] = leaf_acc[leaf, qc] - fold_rows(taken)

    onward = (above, below)
    turns = (1, -1)
    lean = 2 * (z % 2) - 1

    def quarter_step(leaf, step):
        shift = (0, lean, -lean, 2)[step]
        quarter(leaf, ((z + 4) // 2 + shift + 8) % 4)

    def mine(leaf, number, piece):
        return contrib.at[leaf, number // 2, number % 2, piece]

    def place(leaf, number, piece):
        block, part = number // 2, number % 2
        row = pl.multiple_of((block // 2) * T + part * (T // 2) + piece * sub, sub)
        col = pl.multiple_of((block % 2) * T, T)
        return face_out.at[leaf, pl.ds(row, sub), pl.ds(col, T)]

    def owner(way, step):
        return (z + turns[way] * (HOPS - step) + Z) % Z

    def scatter_send(way, step, leaf, piece, src):
        push(src, rs_buf.at[way, step, leaf, piece], rs_s.at[way, step, leaf, piece],
             rs_r.at[way, step, leaf, piece], onward[way])

    def scatter_wait(way, step, leaf, piece):
        slot = rs_buf.at[way, step, leaf, piece]
        arrived(slot, rs_s.at[way, step, leaf, piece], rs_r.at[way, step, leaf, piece], onward[way])
        return slot

    def scatter_first(way, step, leaf):
        for piece in range(PIECES):
            scatter_send(way, step, leaf, piece, mine(leaf, owner(way, step), piece))

    def scatter_on(step, leaf, piece, way):
        slot = scatter_wait(way, step - 1, leaf, piece)
        slot[...] = slot[...] + mine(leaf, owner(way, step), piece)[...]
        scatter_send(way, step, leaf, piece, slot)

    def gather_send(way, step, leaf, piece):
        where = place(leaf, (z - turns[way] * step + Z) % Z, piece)
        push(where, where, ag_s.at[way, step, leaf, piece], ag_r.at[way, step, leaf, piece], onward[way])

    def gather_on(step, leaf, piece, way):
        where = place(leaf, (z - turns[way] * (step + 1) + Z) % Z, piece)
        arrived(where, ag_s.at[way, step, leaf, piece], ag_r.at[way, step, leaf, piece], onward[way])
        if step + 1 < HOPS - 1 or (step + 1 < HOPS and way == leaf):
            gather_send(way, step + 1, leaf, piece)

    for leaf in range(2):
        quarter_step(leaf, 0)
        scatter_first(leaf, 0, leaf)
    for leaf in range(2):
        quarter_step(leaf, 1)
        scatter_first(1 - leaf, 1, leaf)
    for leaf in range(2):
        for piece in range(PIECES):
            scatter_on(1, leaf, piece, leaf)
    for step in range(2, HOPS):
        for leaf in range(2):
            quarter_step(leaf, step)
            for piece in range(PIECES):
                for way in range(2):
                    scatter_on(step, leaf, piece, way)

    def small_send(step):
        where = small.at[(z - step + Z) % Z]
        push(where, where, sm_s.at[step], sm_r.at[step], above)

    def small_on(step):
        arrived(small.at[(z - step - 1 + Z) % Z], sm_s.at[step], sm_r.at[step], above)
        if step < Z - 2:
            small_send(step + 1)

    for leaf in range(2):
        for col in range(2):
            row = 2 * leaf + col
            small[z, row : row + 1] = jnp.sum(leaf_acc[leaf, col], axis=0, keepdims=True)
    for k in range(NR):
        root_diagonal(k)
    small_send(0)
    for leaf in range(2):
        for piece in range(PIECES):
            up = scatter_wait(0, HOPS - 1, leaf, piece)
            down = scatter_wait(1, HOPS - 1, leaf, piece)
            place(leaf, z, piece)[...] = up[...] + down[...] + mine(leaf, z, piece)[...]
            for way in range(2):
                gather_send(way, 0, leaf, piece)
    for step in range(HOPS):
        for leaf in range(2):
            for piece in range(PIECES):
                for way in range(2):
                    if step < HOPS - 1 or way == leaf:
                        gather_on(step, leaf, piece, way)
            if 2 * step + leaf < Z - 1:
                small_on(2 * step + leaf)
    total = jnp.sum(small[...], axis=0)
    for leaf in range(2):
        for col in range(2):
            row = 2 * leaf + col
            leaf_out[leaf : leaf + 1, col * T : (col + 1) * T] = total[row : row + 1]
    root_row = jnp.zeros((1, T), F32)
    for k in range(NR):
        root_row = root_row + jnp.where(y == k, total[4 + k : 5 + k], 0.0)
    root_row = pltpu.roll(root_row, (T - (x * 2 + core) * band) % T, 1)
    root_out[...] = root_row[:, :128]
    for copy in sent:
        copy.wait_send()


def per_device(pole_weight, root_factor, leaf_factor, leaf_upper, leaf_lower, face_tiles):
    T = root_factor.shape[-1] // NR
    band = root_factor.shape[2]
    wide = 2 * T
    whole = pl.BlockSpec(memory_space=pl.ANY)
    scalars = pl.BlockSpec(memory_space=pltpu.SMEM)
    vmem = pl.BlockSpec(memory_space=pltpu.VMEM)
    dma = pltpu.SemaphoreType.DMA
    face, leaf, root = pl.pallas_call(
        functools.partial(kernel, T),
        out_shape=(
            pltpu.VMEM((2, wide, wide), F32),
            pltpu.VMEM((2, wide), F32),
            pltpu.VMEM((1, 128), F32),
        ),
        in_specs=[scalars, scalars, whole, whole, whole, whole],
        out_specs=(vmem, vmem, vmem),
        scratch_shapes=[
            pltpu.VMEM((2, Y, X, 2, band, NR * T), F32),
            pltpu.VMEM((2, NR, NR, T, T), BF16),
            pltpu.VMEM((2, NR, NR, T, T), BF16),
            pltpu.VMEM((2, NR, NR, T, T), BF16),
            pltpu.VMEM((2, NR, NR, T, T), BF16),
            pltpu.VMEM((2, 2, wide, wide), F32),
            pltpu.VMEM((2, 2, wide, wide), F32),
            pltpu.VMEM((2, 2, wide, wide), F32),
            pltpu.VMEM((2, 2, wide, wide), F32),
            pltpu.VMEM((2, 2, wide, wide), BF16),
            pltpu.VMEM((2, 2, wide, wide), BF16),
            pltpu.VMEM((NR, 2, T, T), F32),
            pltpu.VMEM((2, 4, 2, PIECES, T // 2 // PIECES, T), F32),
            pltpu.VMEM((2, HOPS, 2, PIECES, T // 2 // PIECES, T), F32),
            pltpu.VMEM((2, 2, 8, T), F32),
            pltpu.VMEM((Z, 8, T), F32),
            dma((4,)),
            dma((2, 2, 4)), dma((2, 2, 4)),
            dma((2, 4, NR, 4)), dma((2, 4, NR, 4)),
            dma((2, 4, NR)), dma((2, 4, NR)),
            dma((2, HOPS, 2, PIECES)), dma((2, HOPS, 2, PIECES)),
            dma((2, HOPS, 2, PIECES)), dma((2, HOPS, 2, PIECES)),
            dma((Z - 1,)), dma((Z - 1,)),
        ],
        compiler_params=pltpu.CompilerParams(
            collective_id=0, has_side_effects=True, vmem_limit_bytes=60 * 1024 * 1024
        ),
    )(pole_weight, face_tiles, root_factor[0], leaf_factor[0], leaf_upper[0], leaf_lower[0])
    return root[0, :band], leaf, face


def solution(mesh):
    return jax.shard_map(
        per_device,
        mesh=mesh,
        in_specs=(
            P("pole", None),
            P("pole", None, "snode", None),
            P("pole", "snode", None, None, None),
            P("pole", "snode", None, None, None),
            P("pole", "snode", None, None, None),
            P("snode", None),
        ),
        out_specs=(P("snode"), P("snode", None), P("snode", None, None)),
        check_vma=False,
    )
```

```python
import functools

import jax
import jax.numpy as jnp
from jax import lax
from jax.experimental import pallas as pl
from jax.experimental.pallas import tpu as pltpu
from jax.sharding import PartitionSpec as P

NR = 4
X = 4
Y = 4
Z = 8
HOPS = Z // 2
PIECES = 2
F32 = jnp.float32
BF16 = jnp.bfloat16


def split(value):
    high = value.astype(BF16)
    return high, (value - high.astype(F32)).astype(BF16)


def product(left, right):
    def three(a, b):
        ah, al = (jnp.concatenate([item[n] for item in left], 1) for n in (a, a + 1))
        bh, bl = (jnp.concatenate([item[n] for item in right], 0) for n in (b, b + 1))
        return jnp.dot(
            jnp.concatenate([ah, ah, al], 1), jnp.concatenate([bh, bl, bh], 0), preferred_element_type=F32
        )

    return jnp.concatenate([three(0, 0) - three(2, 2), three(0, 2) + three(2, 0)], 0)


def fold_rows(value):
    rows, cols = value.shape
    return jnp.sum(value.reshape(rows // 8, 8, cols), axis=0)


def kernel(
    T,
    w_ref, faces_ref, root_hbm, lf_hbm, lu_hbm, ll_hbm,
    face_out, leaf_out, root_out,
    root_all, fh, fl, gh, gl, lf, lu, lut, ll, lh, lo, pivots, given, taken, contrib, rs_buf, leaf_acc, small,
    in_sem, p1_s, p1_r, p2_s, p2_r, sib_s, sib_r, rs_s, rs_r, ag_s, ag_r, sm_s, sm_r, ex_s, ex_r,
):
    z = lax.axis_index("pole")
    s = lax.axis_index("snode")
    core = s % 2
    x = (s // 2) % X
    y = s // (2 * X)
    band = root_hbm.shape[1]
    half = band // 2
    sub = T // 2 // PIECES

    def at_xy(yy, xx, cc):
        return {"snode": (yy * X + xx) * 2 + cc}

    turn = 1 - 2 * core
    xp, xm, x2 = (x + turn + X) % X, (x - turn + X) % X, (x + 2) % X
    yp, ym, y2 = (y + turn + Y) % Y, (y - turn + Y) % Y, (y + 2) % Y
    zp, zm = (z + turn + Z) % Z, (z - turn + Z) % Z
    east, west = at_xy(y, xp, core), at_xy(y, xm, core)
    north, south = at_xy(yp, x, core), at_xy(ym, x, core)
    mate = at_xy(y, x, 1 - core)
    above, below = {"pole": zp}, {"pole": zm}

    def remote(src, dst, send, recv, to):
        return pltpu.make_async_remote_copy(
            src_ref=src, dst_ref=dst, send_sem=send, recv_sem=recv,
            device_id=to, device_id_type=pl.DeviceIdType.MESH,
        )

    sent = []

    def push(src, dst, send, recv, to):
        copy = remote(src, dst, send, recv, to)
        copy.start()
        sent.append(copy)

    def drain():
        for copy in sent:
            copy.wait_send()
        sent.clear()

    def arrived(dst, send, recv, to):
        remote(dst, dst, send, recv, to).wait_recv()

    barrier = pltpu.get_barrier_semaphore()
    for to in (east, west, north, south, mate, above, below):
        pl.semaphore_signal(barrier, inc=1, device_id=to, device_id_type=pl.DeviceIdType.MESH)

    loads = [
        pltpu.make_async_copy(root_hbm, root_all.at[:, y, x, core], in_sem.at[0]),
        pltpu.make_async_copy(lf_hbm, lf, in_sem.at[1]),
        pltpu.make_async_copy(lu_hbm, lu, in_sem.at[2]),
        pltpu.make_async_copy(ll_hbm, ll, in_sem.at[3]),
    ]
    loads[0].start()
    pl.semaphore_wait(barrier, 7)

    everything = slice(None)
    fore, rear = pl.ds(0, half), pl.ds(half, half)
    halves = (pl.ds(2 * T, 2 * T), pl.ds(0, 2 * T))
    tiles = [pl.ds(wave * T, T) for wave in range(NR)]
    along = ((y, ym, yp, y2), (x, xm, xp, x2))
    across = ((x, xm, xp, x2), (y, ym, yp, y2))
    first_ways = ((east, west), (north, south))
    second_ways = ((north, south), (east, west))

    def spot(part, line, cross, rows, cols, other=core):
        if part == 0:
            return root_all.at[0, line, cross, other, rows, cols]
        return root_all.at[1, cross, line, other, rows, cols]

    def line_send(part, h):
        for number, to in enumerate(first_ways[part]):
            push(root_hbm.at[part, :, halves[h]], spot(part, along[part][0], across[part][0], everything, halves[h]),
                 p1_s.at[part, h, number], p1_r.at[part, h, number], to)

    def line_near(part, h):
        for number, to in enumerate(first_ways[part]):
            cross = across[part][1 + number]
            arrived(spot(part, along[part][0], cross, everything, halves[h]),
                    p1_s.at[part, h, number], p1_r.at[part, h, number], to)
            piece = spot(part, along[part][0], cross, (fore, rear)[number], halves[h])
            push(piece, piece, p1_s.at[part, h, 2 + number], p1_r.at[part, h, 2 + number], to)

    def line_far(part, h):
        for number, to in enumerate(first_ways[part]):
            arrived(spot(part, along[part][0], across[part][3], (fore, rear)[number], halves[h]),
                    p1_s.at[part, h, 2 + number], p1_r.at[part, h, 2 + number], to)

    def near_send(part, group, cut):
        cols = (halves if group == 0 else tiles)[cut]
        for number, to in enumerate(second_ways[part]):
            piece = spot(part, along[part][0], across[part][group], everything, cols)
            src = root_hbm.at[part, :, cols] if group == 0 else piece
            push(src, piece, p2_s.at[part, group, cut, number], p2_r.at[part, group, cut, number], to)

    def far_rows(group, number):
        if group in (0, 3):
            return (fore, rear)[number]
        return everything if group == 1 + number else None

    def near_in(part, group, cut):
        cols = (halves if group == 0 else tiles)[cut]
        for number, to in enumerate(second_ways[part]):
            line = along[part][1 + number]
            arrived(spot(part, line, across[part][group], everything, cols),
                    p2_s.at[part, group, cut, number], p2_r.at[part, group, cut, number], to)
            rows = far_rows(group, number)
            if rows is not None:
                piece = spot(part, line, across[part][group], rows, cols)
                push(piece, piece, p2_s.at[part, group, cut, 2 + number],
                     p2_r.at[part, group, cut, 2 + number], to)

    def far_in(part, group, cut):
        cols = (halves if group == 0 else tiles)[cut]
        for number, to in enumerate(second_ways[part]):
            rows = far_rows(group, number)
            if rows is not None:
                arrived(spot(part, along[part][3], across[part][group], rows, cols),
                        p2_s.at[part, group, cut, 2 + number], p2_r.at[part, group, cut, 2 + number], to)

    parts = (0, 1)

    def mate_lines(cut, numbers, cols, other):
        for part in parts:
            for number in numbers:
                yield part, number, spot(part, along[part][number], everything, everything, cols, other)

    def to_mate(cut, numbers, cols):
        for part, number, piece in mate_lines(cut, numbers, cols, core):
            push(piece, piece, sib_s.at[part, number, cut], sib_r.at[part, number, cut], mate)

    def from_mate(cut, numbers, cols):
        for part, number, piece in mate_lines(cut, numbers, cols, 1 - core):
            arrived(piece, sib_s.at[part, number, cut], sib_r.at[part, number, cut], mate)

    def relay_near(wave):
        for group in (1, 2, 3):
            for part in parts:
                near_in(part, group, wave)
        to_mate(wave, (1, 2), tiles[wave])

    def relay_far(wave):
        for group in (1, 2, 3):
            for part in parts:
                far_in(part, group, wave)
        to_mate(wave, (3,), tiles[wave])

    def waves_send(wave, groups):
        for group in groups:
            for part in parts:
                near_send(part, group, wave)

    def own_part(action, h):
        for part in parts:
            action(part, 0, h)

    def line_part(action, h):
        for part in parts:
            action(part, h)

    def own_line(h):
        to_mate(h, (0,), halves[h])

    def mate_line(h):
        from_mate(h, (0,), halves[h])

    line_part(line_send, 0)
    own_part(near_send, 0)
    for load in loads[1:]:
        load.start()

    wr = w_ref[0, 0]
    wi = w_ref[0, 1]
    own_col = 3 - core
    eye = (
        lax.broadcasted_iota(jnp.int32, (T, T), 0) == lax.broadcasted_iota(jnp.int32, (T, T), 1)
    ).astype(F32)

    def weighted_diagonal(real, imag):
        return jnp.sum(fold_rows((wr * real - wi * imag) * eye), axis=0, keepdims=True)

    first, second = pl.ds(0, T), pl.ds(T, T)

    def leaf_inverse(leaf):
        pr, pi = lf[leaf, 0, second, second], lf[leaf, 1, second, second]
        inner = product(
            [split(pr) + split(pi)],
            [split(lf[leaf, 0, second, first]) + split(lf[leaf, 1, second, first])],
        )
        ur, ui = lf[leaf, 0, first, second].T, lf[leaf, 1, first, second].T
        tr, ti = inner[:T], inner[T:]
        total = ur * (wr * tr - wi * ti) - ui * (wr * ti + wi * tr)
        base = weighted_diagonal(lf[leaf, 0, first, first], lf[leaf, 1, first, first])
        rows = lax.broadcasted_iota(jnp.int32, (8, T), 0) == 0
        leaf_acc[leaf, 0] = fold_rows(total) + jnp.where(rows, base, 0.0)
        leaf_acc[leaf, 1] = jnp.where(rows, weighted_diagonal(pr, pi), 0.0)

    def turn_upper(leaf):
        for part in range(2):
            for row in (first, second):
                for col in (first, second):
                    lut[leaf, part, col, row] = lu[leaf, part, row, col].T

    def split_lower(leaf):
        for part in range(2):
            for row in (first, second):
                lh[leaf, part, row], lo[leaf, part, row] = split(ll[leaf, part, row])

    def load_wave(wave):
        for part in range(2):
            for row in range(NR):
                if row != wave:
                    tile = root_all[part, row, :, :, :, pl.ds(wave * T, T)].reshape(T, T)
                    fh[part, row, wave], fl[part, row, wave] = split(tile)

    def tile_of(high, lower, row, col):
        return high[0, row, col], lower[0, row, col], high[1, row, col], lower[1, row, col]

    def put(row, col, value):
        gh[0, row, col], gl[0, row, col] = split(value[:T])
        gh[1, row, col], gl[1, row, col] = split(value[T:])

    def upper_part(k, after, col):
        return product([tile_of(fh, fl, k, m) for m in after], [tile_of(gh, gl, m, col) for m in after])

    def uppers(k, cols):
        for col in cols:
            put(k, col, -upper_part(k, range(k + 1, NR), col))

    def hand(number):
        push(given.at[number], taken.at[number], ex_s.at[number], ex_r.at[number], mate)

    def receive(number, row, col):
        arrived(taken.at[number], ex_s.at[number], ex_r.at[number], mate)
        put(row, col, taken[number])

    def own_upper_one():
        value = -upper_part(1, (2, 3), own_col)
        put(1, own_col, value)
        given[0] = value
        hand(0)
        given[1] = upper_part(0, (2, 3), own_col)

    def own_upper_zero():
        value = -(given[1] + upper_part(0, (1,), own_col))
        put(0, own_col, value)
        given[1] = value
        hand(1)

    def own_lower_zero():
        row, after = 3 - core, (1, 2, 3)
        value = -product([tile_of(gh, gl, row, m) for m in after], [tile_of(fh, fl, m, 0) for m in after])
        put(row, 0, value)
        given[2] = value
        hand(2)

    def lowers(rows, k):
        after = range(k + 1, NR)
        for row in rows:
            put(row, k, -product([tile_of(gh, gl, row, m) for m in after], [tile_of(fh, fl, m, k) for m in after]))

    def pivot(k):
        cols = pl.ds(k * T, T)
        real = root_all[0, k, :, :, :, cols].reshape(T, T)
        imag = root_all[1, k, :, :, :, cols].reshape(T, T)
        after = range(k + 1, NR)
        if after:
            lost = product([tile_of(fh, fl, k, m) for m in after], [tile_of(gh, gl, m, k) for m in after])
            real = real - lost[:T]
            imag = imag - lost[T:]
        gh[0, k, k], gl[0, k, k] = split(real)
        gh[1, k, k], gl[1, k, k] = split(imag)
        pivots[k, 0] = real
        pivots[k, 1] = imag

    def root_diagonal(k):
        small[z, 4 + k : 5 + k] = weighted_diagonal(pivots[k, 0], pivots[k, 1])

    loads[1].wait()
    leaf_inverse(0)
    line_part(line_near, 0)
    waves_send(3, (1, 2))
    line_part(line_send, 1)
    waves_send(2, (1, 2))
    leaf_inverse(1)
    line_part(line_far, 0)
    waves_send(3, (3,))
    waves_send(2, (3,))
    loads[0].wait()
    own_line(0)
    own_part(near_send, 1)
    own_part(near_in, 0)
    line_part(line_near, 1)
    loads[3].wait()
    split_lower(0)
    relay_near(3)
    split_lower(1)
    line_part(line_far, 1)
    own_line(1)
    waves_send(1, (1, 2, 3))
    loads[2].wait()
    turn_upper(0)
    relay_near(2)
    own_part(far_in, 0)
    relay_far(3)
    own_part(near_in, 1)
    waves_send(0, (1, 2, 3))
    turn_upper(1)
    mate_line(0)
    from_mate(3, (1, 2, 3), tiles[3])
    load_wave(3)
    pivot(3)
    uppers(2, (3,))
    relay_near(1)
    relay_far(2)
    from_mate(2, (1, 2, 3), tiles[2])
    load_wave(2)
    lowers((3,), 2)
    pivot(2)
    relay_near(0)
    own_part(far_in, 1)
    relay_far(1)
    own_upper_one()
    mate_line(1)
    from_mate(1, (1, 2, 3), tiles[1])
    load_wave(1)
    lowers((3, 2), 1)
    relay_far(0)
    pivot(1)
    own_upper_zero()
    uppers(0, (1,))
    from_mate(0, (1, 2, 3), tiles[0])
    load_wave(0)
    receive(0, 1, 2 + core)
    own_lower_zero()
    lowers((1,), 0)
    receive(2, 2 + core, 0)
    pivot(0)
    receive(1, 0, 2 + core)

    def quarter(leaf, number):
        qr, qc = number // 2, number % 2
        cols = pl.ds(pl.multiple_of(qc * T, T), T)
        row = faces_ref[leaf, qr]
        lefts, rights = [], []
        for face in range(2):
            col = faces_ref[leaf, face]
            lefts.append(tile_of(gh, gl, row, col))
            inner = pl.ds(face * T, T)
            rights.append((lh[leaf, 0, inner, cols], lo[leaf, 0, inner, cols],
                           lh[leaf, 1, inner, cols], lo[leaf, 1, inner, cols]))
        block = -product(lefts, rights)
        real, imag = block[:T], block[T:]
        dr = wr * real - wi * imag
        di = wr * imag + wi * real
        contrib[leaf, number] = dr.reshape(2, PIECES, sub, T)
        rows = pl.ds(pl.multiple_of(qr * T, T), T)
        lost = lut[leaf, 0, rows, cols] * dr - lut[leaf, 1, rows, cols] * di
        leaf_acc[leaf, qc] = leaf_acc[leaf, qc] - fold_rows(lost)

    onward = (above, below)
    turns = (turn, -turn)
    lean = 2 * (z % 2) - 1

    def quarter_step(leaf, step):
        shift = (0, lean, -lean, 2)[step]
        quarter(leaf, ((z + 4) // 2 + shift + 8) % 4)

    def mine(leaf, number, piece):
        return contrib.at[leaf, number // 2, number % 2, piece]

    def place(leaf, number, piece):
        block, part = number // 2, number % 2
        row = pl.multiple_of((block // 2) * T + part * (T // 2) + piece * sub, sub)
        col = pl.multiple_of((block % 2) * T, T)
        return face_out.at[leaf, pl.ds(row, sub), pl.ds(col, T)]

    def owner(way, step):
        return (z + turns[way] * (HOPS - step) + Z) % Z

    def scatter_send(way, step, leaf, piece, src):
        push(src, rs_buf.at[way, step, leaf, piece], rs_s.at[way, step, leaf, piece],
             rs_r.at[way, step, leaf, piece], onward[way])

    def scatter_wait(way, step, leaf, piece):
        slot = rs_buf.at[way, step, leaf, piece]
        arrived(slot, rs_s.at[way, step, leaf, piece], rs_r.at[way, step, leaf, piece], onward[way])
        return slot

    def scatter_first(way, step, leaf):
        for piece in range(PIECES):
            scatter_send(way, step, leaf, piece, mine(leaf, owner(way, step), piece))

    def scatter_on(step, leaf, piece, way):
        slot = scatter_wait(way, step - 1, leaf, piece)
        slot[...] = slot[...] + mine(leaf, owner(way, step), piece)[...]
        scatter_send(way, step, leaf, piece, slot)

    def gather_send(way, step, leaf, piece):
        where = place(leaf, (z - turns[way] * step + Z) % Z, piece)
        push(where, where, ag_s.at[way, step, leaf, piece], ag_r.at[way, step, leaf, piece], onward[way])

    def gather_on(step, leaf, piece, way):
        where = place(leaf, (z - turns[way] * (step + 1) + Z) % Z, piece)
        arrived(where, ag_s.at[way, step, leaf, piece], ag_r.at[way, step, leaf, piece], onward[way])
        if step + 1 < HOPS - 1 or (step + 1 < HOPS and way == leaf):
            gather_send(way, step + 1, leaf, piece)

    earlier = sent[:]
    sent.clear()
    for leaf in range(2):
        quarter_step(leaf, 0)
        scatter_first(leaf, 0, leaf)
    for leaf in range(2):
        quarter_step(leaf, 1)
        scatter_first(1 - leaf, 1, leaf)
    for copy in earlier:
        copy.wait_send()
    for leaf in range(2):
        for piece in range(PIECES):
            scatter_on(1, leaf, piece, leaf)
    for step in range(2, HOPS):
        for leaf in range(2):
            quarter_step(leaf, step)
            for piece in range(PIECES):
                for way in range(2):
                    scatter_on(step, leaf, piece, way)

    def small_send(step):
        where = small.at[(z - turn * step + Z) % Z]
        push(where, where, sm_s.at[step], sm_r.at[step], above)

    def small_on(step):
        arrived(small.at[(z - turn * (step + 1) + Z) % Z], sm_s.at[step], sm_r.at[step], above)
        if step < Z - 2:
            small_send(step + 1)

    for leaf in range(2):
        for col in range(2):
            row = 2 * leaf + col
            small[z, row : row + 1] = jnp.sum(leaf_acc[leaf, col], axis=0, keepdims=True)
    for k in range(NR):
        root_diagonal(k)
    small_send(0)
    for leaf in range(2):
        for piece in range(PIECES):
            up = scatter_wait(0, HOPS - 1, leaf, piece)
            down = scatter_wait(1, HOPS - 1, leaf, piece)
            place(leaf, z, piece)[...] = up[...] + down[...] + mine(leaf, z, piece)[...]
            for way in range(2):
                gather_send(way, 0, leaf, piece)
    scattered = sent[:]
    sent.clear()
    for step in range(HOPS):
        if step == 2:
            for copy in scattered:
                copy.wait_send()
        for leaf in range(2):
            for piece in range(PIECES):
                for way in range(2):
                    if step < HOPS - 1 or way == leaf:
                        gather_on(step, leaf, piece, way)
            if 2 * step + leaf < Z - 1:
                small_on(2 * step + leaf)
    total = jnp.sum(small[...], axis=0)
    for leaf in range(2):
        for col in range(2):
            row = 2 * leaf + col
            leaf_out[leaf : leaf + 1, col * T : (col + 1) * T] = total[row : row + 1]
    root_row = jnp.zeros((1, T), F32)
    for k in range(NR):
        root_row = root_row + jnp.where(y == k, total[4 + k : 5 + k], 0.0)
    root_row = pltpu.roll(root_row, (T - (x * 2 + core) * band) % T, 1)
    root_out[...] = root_row[:, :128]
    drain()


def per_device(pole_weight, root_factor, leaf_factor, leaf_upper, leaf_lower, face_tiles):
    T = root_factor.shape[-1] // NR
    band = root_factor.shape[2]
    wide = 2 * T
    whole = pl.BlockSpec(memory_space=pl.ANY)
    scalars = pl.BlockSpec(memory_space=pltpu.SMEM)
    vmem = pl.BlockSpec(memory_space=pltpu.VMEM)
    dma = pltpu.SemaphoreType.DMA
    face, leaf, root = pl.pallas_call(
        functools.partial(kernel, T),
        out_shape=(
            pltpu.VMEM((2, wide, wide), F32),
            pltpu.VMEM((2, wide), F32),
            pltpu.VMEM((1, 128), F32),
        ),
        in_specs=[scalars, scalars, whole, whole, whole, whole],
        out_specs=(vmem, vmem, vmem),
        scratch_shapes=[
            pltpu.VMEM((2, Y, X, 2, band, NR * T), F32),
            pltpu.VMEM((2, NR, NR, T, T), BF16),
            pltpu.VMEM((2, NR, NR, T, T), BF16),
            pltpu.VMEM((2, NR, NR, T, T), BF16),
            pltpu.VMEM((2, NR, NR, T, T), BF16),
            pltpu.VMEM((2, 2, wide, wide), F32),
            pltpu.VMEM((2, 2, wide, wide), F32),
            pltpu.VMEM((2, 2, wide, wide), F32),
            pltpu.VMEM((2, 2, wide, wide), F32),
            pltpu.VMEM((2, 2, wide, wide), BF16),
            pltpu.VMEM((2, 2, wide, wide), BF16),
            pltpu.VMEM((NR, 2, T, T), F32),
            pltpu.VMEM((3, 2 * T, T), F32),
            pltpu.VMEM((3, 2 * T, T), F32),
            pltpu.VMEM((2, 4, 2, PIECES, T // 2 // PIECES, T), F32),
            pltpu.VMEM((2, HOPS, 2, PIECES, T // 2 // PIECES, T), F32),
            pltpu.VMEM((2, 2, 8, T), F32),
            pltpu.VMEM((Z, 8, T), F32),
            dma((4,)),
            dma((2, 2, 4)), dma((2, 2, 4)),
            dma((2, 4, NR, 4)), dma((2, 4, NR, 4)),
            dma((2, 4, NR)), dma((2, 4, NR)),
            dma((2, HOPS, 2, PIECES)), dma((2, HOPS, 2, PIECES)),
            dma((2, HOPS, 2, PIECES)), dma((2, HOPS, 2, PIECES)),
            dma((Z - 1,)), dma((Z - 1,)),
            dma((3,)), dma((3,)),
        ],
        compiler_params=pltpu.CompilerParams(
            collective_id=0, has_side_effects=True, vmem_limit_bytes=60 * 1024 * 1024
        ),
    )(pole_weight, face_tiles, root_factor[0], leaf_factor[0], leaf_upper[0], leaf_lower[0])
    return root[0, :band], leaf, face


def solution(mesh):
    return jax.shard_map(
        per_device,
        mesh=mesh,
        in_specs=(
            P("pole", None),
            P("pole", None, "snode", None),
            P("pole", "snode", None, None, None),
            P("pole", "snode", None, None, None),
            P("pole", "snode", None, None, None),
            P("snode", None),
        ),
        out_specs=(P("snode"), P("snode", None), P("snode", None, None)),
        check_vma=False,
    )
```

```python
import functools

import jax
import jax.numpy as jnp
from jax import lax
from jax.experimental import pallas as pl
from jax.experimental.pallas import tpu as pltpu
from jax.sharding import PartitionSpec as P

NR = 4
X = 4
Y = 4
Z = 8
HOPS = Z // 2
PIECES = 2
F32 = jnp.float32
BF16 = jnp.bfloat16


def split(value):
    high = value.astype(BF16)
    return high, (value - high.astype(F32)).astype(BF16)


def product(left, right):
    def three(a, b):
        ah, al = (jnp.concatenate([item[n] for item in left], 1) for n in (a, a + 1))
        bh, bl = (jnp.concatenate([item[n] for item in right], 0) for n in (b, b + 1))
        return jnp.dot(
            jnp.concatenate([ah, ah, al], 1), jnp.concatenate([bh, bl, bh], 0), preferred_element_type=F32
        )

    return jnp.concatenate([three(0, 0) - three(2, 2), three(0, 2) + three(2, 0)], 0)


def fold_rows(value):
    rows, cols = value.shape
    return jnp.sum(value.reshape(rows // 8, 8, cols), axis=0)


def kernel(
    T,
    w_ref, faces_ref, root_hbm, lf_hbm, lu_hbm, ll_hbm,
    face_out, leaf_out, root_out,
    root_all, fh, fl, gh, gl, lf, lu, lut, ll, lh, lo, pivots, given, taken, imags, contrib, rs_buf, leaf_acc, small,
    in_sem, p1_s, p1_r, p2_s, p2_r, sib_s, sib_r, rs_s, rs_r, ag_s, ag_r, sm_s, sm_r, ex_s, ex_r,
):
    z = lax.axis_index("pole")
    s = lax.axis_index("snode")
    core = s % 2
    x = (s // 2) % X
    y = s // (2 * X)
    band = root_hbm.shape[1]
    half = band // 2
    sub = T // 2 // PIECES

    def at_xy(yy, xx, cc):
        return {"snode": (yy * X + xx) * 2 + cc}

    turn = 1 - 2 * core
    xp, xm, x2 = (x + turn + X) % X, (x - turn + X) % X, (x + 2) % X
    yp, ym, y2 = (y + turn + Y) % Y, (y - turn + Y) % Y, (y + 2) % Y
    zp, zm = (z + turn + Z) % Z, (z - turn + Z) % Z
    east, west = at_xy(y, xp, core), at_xy(y, xm, core)
    north, south = at_xy(yp, x, core), at_xy(ym, x, core)
    mate = at_xy(y, x, 1 - core)
    above, below = {"pole": zp}, {"pole": zm}

    def remote(src, dst, send, recv, to):
        return pltpu.make_async_remote_copy(
            src_ref=src, dst_ref=dst, send_sem=send, recv_sem=recv,
            device_id=to, device_id_type=pl.DeviceIdType.MESH,
        )

    sent = []

    def push(src, dst, send, recv, to):
        copy = remote(src, dst, send, recv, to)
        copy.start()
        sent.append(copy)

    def drain():
        for copy in sent:
            copy.wait_send()
        sent.clear()

    def arrived(dst, send, recv, to):
        remote(dst, dst, send, recv, to).wait_recv()

    barrier = pltpu.get_barrier_semaphore()
    for to in (east, west, north, south, mate, above, below):
        pl.semaphore_signal(barrier, inc=1, device_id=to, device_id_type=pl.DeviceIdType.MESH)

    loads = [
        pltpu.make_async_copy(root_hbm, root_all.at[:, y, x, core], in_sem.at[0]),
        pltpu.make_async_copy(lf_hbm, lf, in_sem.at[1]),
        pltpu.make_async_copy(lu_hbm, lu, in_sem.at[2]),
        pltpu.make_async_copy(ll_hbm, ll, in_sem.at[3]),
    ]
    for load in loads:
        load.start()
    pl.semaphore_wait(barrier, 7)

    everything = slice(None)
    fore, rear = pl.ds(0, half), pl.ds(half, half)
    halves = (pl.ds(2 * T, 2 * T), pl.ds(0, 2 * T))
    tiles = [pl.ds(wave * T, T) for wave in range(NR)]
    along = ((y, ym, yp, y2), (x, xm, xp, x2))
    across = ((x, xm, xp, x2), (y, ym, yp, y2))
    first_ways = ((east, west), (north, south))
    second_ways = ((north, south), (east, west))

    def spot(part, line, cross, rows, cols, other=core):
        if part == 0:
            return root_all.at[0, line, cross, other, rows, cols]
        return root_all.at[1, cross, line, other, rows, cols]

    def line_send(part, h):
        for number, to in enumerate(first_ways[part]):
            push(spot(part, along[part][0], across[part][0], everything, halves[h]),
                 spot(part, along[part][0], across[part][0], everything, halves[h]),
                 p1_s.at[part, h, number], p1_r.at[part, h, number], to)

    def line_near(part, h):
        for number, to in enumerate(first_ways[part]):
            cross = across[part][1 + number]
            arrived(spot(part, along[part][0], cross, everything, halves[h]),
                    p1_s.at[part, h, number], p1_r.at[part, h, number], to)
            piece = spot(part, along[part][0], cross, (fore, rear)[number], halves[h])
            push(piece, piece, p1_s.at[part, h, 2 + number], p1_r.at[part, h, 2 + number], to)

    def line_far(part, h):
        for number, to in enumerate(first_ways[part]):
            arrived(spot(part, along[part][0], across[part][3], (fore, rear)[number], halves[h]),
                    p1_s.at[part, h, 2 + number], p1_r.at[part, h, 2 + number], to)

    def near_send(part, group, cut):
        cols = (halves if group == 0 else tiles)[cut]
        for number, to in enumerate(second_ways[part]):
            piece = spot(part, along[part][0], across[part][group], everything, cols)
            push(piece, piece, p2_s.at[part, group, cut, number], p2_r.at[part, group, cut, number], to)

    def far_rows(group, number):
        if group in (0, 3):
            return (fore, rear)[number]
        return everything if group == 1 + number else None

    def near_in(part, group, cut):
        cols = (halves if group == 0 else tiles)[cut]
        for number, to in enumerate(second_ways[part]):
            line = along[part][1 + number]
            arrived(spot(part, line, across[part][group], everything, cols),
                    p2_s.at[part, group, cut, number], p2_r.at[part, group, cut, number], to)
            rows = far_rows(group, number)
            if rows is not None:
                piece = spot(part, line, across[part][group], rows, cols)
                push(piece, piece, p2_s.at[part, group, cut, 2 + number],
                     p2_r.at[part, group, cut, 2 + number], to)

    def far_in(part, group, cut):
        cols = (halves if group == 0 else tiles)[cut]
        for number, to in enumerate(second_ways[part]):
            rows = far_rows(group, number)
            if rows is not None:
                arrived(spot(part, along[part][3], across[part][group], rows, cols),
                        p2_s.at[part, group, cut, 2 + number], p2_r.at[part, group, cut, 2 + number], to)

    parts = (0, 1)

    def mate_lines(cut, numbers, cols, other):
        for part in parts:
            for number in numbers:
                yield part, number, spot(part, along[part][number], everything, everything, cols, other)

    def to_mate(cut, numbers, cols):
        for part, number, piece in mate_lines(cut, numbers, cols, core):
            push(piece, piece, sib_s.at[part, number, cut], sib_r.at[part, number, cut], mate)

    def from_mate(cut, numbers, cols):
        for part, number, piece in mate_lines(cut, numbers, cols, 1 - core):
            arrived(piece, sib_s.at[part, number, cut], sib_r.at[part, number, cut], mate)

    def relay_near(wave):
        for group in (1, 2, 3):
            for part in parts:
                near_in(part, group, wave)
        to_mate(wave, (1, 2), tiles[wave])

    def relay_far(wave):
        for group in (1, 2, 3):
            for part in parts:
                far_in(part, group, wave)
        to_mate(wave, (3,), tiles[wave])

    def waves_send(wave, groups):
        for group in groups:
            for part in parts:
                near_send(part, group, wave)

    def own_part(action, h):
        for part in parts:
            action(part, 0, h)

    def line_part(action, h):
        for part in parts:
            action(part, h)

    def own_line(h):
        to_mate(h, (0,), halves[h])

    def mate_line(h):
        from_mate(h, (0,), halves[h])

    loads[0].wait()
    line_part(line_send, 0)
    own_part(near_send, 0)

    wr = w_ref[0, 0]
    wi = w_ref[0, 1]
    own_col = 3 - core
    edge = T // 2
    eye = (
        lax.broadcasted_iota(jnp.int32, (edge, edge), 0) == lax.broadcasted_iota(jnp.int32, (edge, edge), 1)
    )

    def weighted_diagonal(real, imag):
        found = []
        for begin in (0, edge):
            block = (slice(begin, begin + edge),) * 2
            found.append(fold_rows(jnp.where(eye, wr * real[block] - wi * imag[block], 0.0)))
        return jnp.sum(jnp.concatenate(found, 1), axis=0, keepdims=True)

    first, second = pl.ds(0, T), pl.ds(T, T)

    def leaf_inverse(leaf):
        pr, pi = lf[leaf, 0, second, second], lf[leaf, 1, second, second]
        inner = product(
            [split(pr) + split(pi)],
            [split(lf[leaf, 0, second, first]) + split(lf[leaf, 1, second, first])],
        )
        ur, ui = lf[leaf, 0, first, second].T, lf[leaf, 1, first, second].T
        tr, ti = inner[:T], inner[T:]
        total = ur * (wr * tr - wi * ti) - ui * (wr * ti + wi * tr)
        base = weighted_diagonal(lf[leaf, 0, first, first], lf[leaf, 1, first, first])
        rows = lax.broadcasted_iota(jnp.int32, (8, T), 0) == 0
        leaf_acc[leaf, 0] = fold_rows(total) + jnp.where(rows, base, 0.0)
        leaf_acc[leaf, 1] = jnp.where(rows, weighted_diagonal(pr, pi), 0.0)

    def turn_upper(leaf):
        for part in range(2):
            for row in (first, second):
                for col in (first, second):
                    lut[leaf, part, col, row] = lu[leaf, part, row, col].T

    def split_lower(leaf):
        for part in range(2):
            for row in (first, second):
                lh[leaf, part, row], lo[leaf, part, row] = split(ll[leaf, part, row])

    def load_wave(wave):
        for part in range(2):
            for row in range(NR):
                if row != wave:
                    tile = root_all[part, row, :, :, :, pl.ds(wave * T, T)].reshape(T, T)
                    fh[part, row, wave], fl[part, row, wave] = split(tile)

    def tile_of(high, lower, row, col):
        return high[0, row, col], lower[0, row, col], high[1, row, col], lower[1, row, col]

    def put(row, col, value):
        gh[0, row, col], gl[0, row, col] = split(value[:T])
        gh[1, row, col], gl[1, row, col] = split(value[T:])

    def upper_part(k, after, col):
        return product([tile_of(fh, fl, k, m) for m in after], [tile_of(gh, gl, m, col) for m in after])

    def uppers(k, cols):
        for col in cols:
            put(k, col, -upper_part(k, range(k + 1, NR), col))

    def hand(number):
        push(given.at[number], taken.at[number], ex_s.at[number], ex_r.at[number], mate)

    def receive(number, row, col):
        arrived(taken.at[number], ex_s.at[number], ex_r.at[number], mate)
        put(row, col, taken[number])

    def own_upper_one():
        value = -upper_part(1, (2, 3), own_col)
        put(1, own_col, value)
        given[0] = value
        hand(0)
        given[1] = upper_part(0, (2, 3), own_col)

    def own_upper_zero():
        value = -(given[1] + upper_part(0, (1,), own_col))
        put(0, own_col, value)
        given[1] = value
        hand(1)

    def own_lower_zero():
        row, after = 3 - core, (1, 2, 3)
        value = -product([tile_of(gh, gl, row, m) for m in after], [tile_of(fh, fl, m, 0) for m in after])
        put(row, 0, value)
        given[2] = value
        hand(2)

    def lowers(rows, k):
        after = range(k + 1, NR)
        for row in rows:
            put(row, k, -product([tile_of(gh, gl, row, m) for m in after], [tile_of(fh, fl, m, k) for m in after]))

    def pivot(k):
        cols = pl.ds(k * T, T)
        real = root_all[0, k, :, :, :, cols].reshape(T, T)
        imag = root_all[1, k, :, :, :, cols].reshape(T, T)
        after = range(k + 1, NR)
        if after:
            lost = product([tile_of(fh, fl, k, m) for m in after], [tile_of(gh, gl, m, k) for m in after])
            real = real - lost[:T]
            imag = imag - lost[T:]
        gh[0, k, k], gl[0, k, k] = split(real)
        gh[1, k, k], gl[1, k, k] = split(imag)
        pivots[k, 0] = real
        pivots[k, 1] = imag

    def root_diagonal(k):
        small[z, 4 + k : 5 + k] = weighted_diagonal(pivots[k, 0], pivots[k, 1])

    loads[1].wait()
    leaf_inverse(0)
    line_part(line_near, 0)
    waves_send(3, (1, 2))
    line_part(line_send, 1)
    waves_send(2, (1, 2))
    leaf_inverse(1)
    line_part(line_far, 0)
    waves_send(3, (3,))
    waves_send(2, (3,))
    own_line(0)
    own_part(near_send, 1)
    own_part(near_in, 0)
    line_part(line_near, 1)
    loads[3].wait()
    split_lower(0)
    relay_near(3)
    split_lower(1)
    line_part(line_far, 1)
    own_line(1)
    waves_send(1, (1, 2, 3))
    loads[2].wait()
    turn_upper(0)
    relay_near(2)
    own_part(far_in, 0)
    relay_far(3)
    own_part(near_in, 1)
    waves_send(0, (1, 2, 3))
    turn_upper(1)
    mate_line(0)
    from_mate(3, (1, 2, 3), tiles[3])
    load_wave(3)
    pivot(3)
    uppers(2, (3,))
    relay_near(1)
    relay_far(2)
    from_mate(2, (1, 2, 3), tiles[2])
    load_wave(2)
    lowers((3,), 2)
    pivot(2)
    relay_near(0)
    own_part(far_in, 1)
    relay_far(1)
    own_upper_one()
    mate_line(1)
    from_mate(1, (1, 2, 3), tiles[1])
    load_wave(1)
    lowers((3, 2), 1)
    relay_far(0)
    pivot(1)
    own_upper_zero()
    uppers(0, (1,))
    receive(0, 1, 2 + core)
    receive(1, 0, 2 + core)
    from_mate(0, (1, 2, 3), tiles[0])
    load_wave(0)
    own_lower_zero()
    lowers((1,), 0)
    receive(2, 2 + core, 0)
    pivot(0)

    def quarter(leaf, number):
        qr, qc = number // 2, number % 2
        cols = pl.ds(pl.multiple_of(qc * T, T), T)
        row = faces_ref[leaf, qr]
        lefts, rights = [], []
        for face in range(2):
            col = faces_ref[leaf, face]
            lefts.append(tile_of(gh, gl, row, col))
            inner = pl.ds(face * T, T)
            rights.append((lh[leaf, 0, inner, cols], lo[leaf, 0, inner, cols],
                           lh[leaf, 1, inner, cols], lo[leaf, 1, inner, cols]))
        block = -product(lefts, rights)
        real, imag = block[:T], block[T:]
        dr = wr * real - wi * imag
        di = wr * imag + wi * real
        contrib[leaf, number] = dr.reshape(2, PIECES, sub, T)
        imags[leaf, number] = di

    def leaf_diagonal(leaf, number):
        qr, qc = number // 2, number % 2
        rows, cols = pl.ds(qr * T, T), pl.ds(qc * T, T)
        dr = contrib[leaf, number].reshape(T, T)
        lost = lut[leaf, 0, rows, cols] * dr - lut[leaf, 1, rows, cols] * imags[leaf, number]
        leaf_acc[leaf, qc] = leaf_acc[leaf, qc] - fold_rows(lost)

    onward = (above, below)
    turns = (turn, -turn)
    lean = 2 * (z % 2) - 1

    def quarter_step(leaf, step):
        shift = (0, lean, -lean, 2)[step]
        quarter(leaf, ((z + 4) // 2 + shift + 8) % 4)

    def mine(leaf, number, piece):
        return contrib.at[leaf, number // 2, number % 2, piece]

    def place(leaf, number, piece):
        block, part = number // 2, number % 2
        row = pl.multiple_of((block // 2) * T + part * (T // 2) + piece * sub, sub)
        col = pl.multiple_of((block % 2) * T, T)
        return face_out.at[leaf, pl.ds(row, sub), pl.ds(col, T)]

    def owner(way, step):
        return (z + turns[way] * (HOPS - step) + Z) % Z

    def scatter_send(way, step, leaf, piece, src):
        push(src, rs_buf.at[way, step, leaf, piece], rs_s.at[way, step, leaf, piece],
             rs_r.at[way, step, leaf, piece], onward[way])

    def scatter_wait(way, step, leaf, piece):
        slot = rs_buf.at[way, step, leaf, piece]
        arrived(slot, rs_s.at[way, step, leaf, piece], rs_r.at[way, step, leaf, piece], onward[way])
        return slot

    def scatter_first(way, step, leaf):
        for piece in range(PIECES):
            scatter_send(way, step, leaf, piece, mine(leaf, owner(way, step), piece))

    def scatter_on(step, leaf, piece, way):
        slot = scatter_wait(way, step - 1, leaf, piece)
        slot[...] = slot[...] + mine(leaf, owner(way, step), piece)[...]
        scatter_send(way, step, leaf, piece, slot)

    def gather_send(way, step, leaf, piece):
        where = place(leaf, (z - turns[way] * step + Z) % Z, piece)
        push(where, where, ag_s.at[way, step, leaf, piece], ag_r.at[way, step, leaf, piece], onward[way])

    def gather_on(step, leaf, piece, way):
        where = place(leaf, (z - turns[way] * (step + 1) + Z) % Z, piece)
        arrived(where, ag_s.at[way, step, leaf, piece], ag_r.at[way, step, leaf, piece], onward[way])
        if step + 1 < HOPS - 1 or (step + 1 < HOPS and way == leaf):
            gather_send(way, step + 1, leaf, piece)

    earlier = sent[:]
    sent.clear()
    for leaf in range(2):
        quarter_step(leaf, 0)
        scatter_first(leaf, 0, leaf)
    for leaf in range(2):
        quarter_step(leaf, 1)
        scatter_first(1 - leaf, 1, leaf)
    for copy in earlier:
        copy.wait_send()
    for leaf in range(2):
        for piece in range(PIECES):
            scatter_on(1, leaf, piece, leaf)
    for step in range(2, HOPS):
        for leaf in range(2):
            quarter_step(leaf, step)
            for piece in range(PIECES):
                for way in range(2):
                    scatter_on(step, leaf, piece, way)

    def small_send(step):
        where = small.at[(z - turn * step + Z) % Z]
        push(where, where, sm_s.at[step], sm_r.at[step], above)

    def small_on(step):
        arrived(small.at[(z - turn * (step + 1) + Z) % Z], sm_s.at[step], sm_r.at[step], above)
        if step < Z - 2:
            small_send(step + 1)

    for leaf in range(2):
        for piece in range(PIECES):
            up = scatter_wait(0, HOPS - 1, leaf, piece)
            down = scatter_wait(1, HOPS - 1, leaf, piece)
            place(leaf, z, piece)[...] = up[...] + down[...] + mine(leaf, z, piece)[...]
            for way in range(2):
                gather_send(way, 0, leaf, piece)
    scattered = sent[:]
    sent.clear()
    for leaf in range(2):
        for number in range(4):
            leaf_diagonal(leaf, number)
    for leaf in range(2):
        for col in range(2):
            row = 2 * leaf + col
            small[z, row : row + 1] = jnp.sum(leaf_acc[leaf, col], axis=0, keepdims=True)
    for k in range(NR):
        root_diagonal(k)
    small_send(0)
    for step in range(HOPS):
        if step == 2:
            for copy in scattered:
                copy.wait_send()
        for leaf in range(2):
            for piece in range(PIECES):
                for way in range(2):
                    if step < HOPS - 1 or way == leaf:
                        gather_on(step, leaf, piece, way)
            if 2 * step + leaf < Z - 1:
                small_on(2 * step + leaf)
    total = jnp.sum(small[...], axis=0)
    for leaf in range(2):
        for col in range(2):
            row = 2 * leaf + col
            leaf_out[leaf : leaf + 1, col * T : (col + 1) * T] = total[row : row + 1]
    root_row = jnp.zeros((1, T), F32)
    for k in range(NR):
        root_row = root_row + jnp.where(y == k, total[4 + k : 5 + k], 0.0)
    root_row = pltpu.roll(root_row, (T - (x * 2 + core) * band) % T, 1)
    root_out[...] = root_row[:, :128]
    drain()


def per_device(pole_weight, root_factor, leaf_factor, leaf_upper, leaf_lower, face_tiles):
    T = root_factor.shape[-1] // NR
    band = root_factor.shape[2]
    wide = 2 * T
    whole = pl.BlockSpec(memory_space=pl.ANY)
    scalars = pl.BlockSpec(memory_space=pltpu.SMEM)
    vmem = pl.BlockSpec(memory_space=pltpu.VMEM)
    dma = pltpu.SemaphoreType.DMA
    face, leaf, root = pl.pallas_call(
        functools.partial(kernel, T),
        out_shape=(
            pltpu.VMEM((2, wide, wide), F32),
            pltpu.VMEM((2, wide), F32),
            pltpu.VMEM((1, 128), F32),
        ),
        in_specs=[scalars, scalars, whole, whole, whole, whole],
        out_specs=(vmem, vmem, vmem),
        scratch_shapes=[
            pltpu.VMEM((2, Y, X, 2, band, NR * T), F32),
            pltpu.VMEM((2, NR, NR, T, T), BF16),
            pltpu.VMEM((2, NR, NR, T, T), BF16),
            pltpu.VMEM((2, NR, NR, T, T), BF16),
            pltpu.VMEM((2, NR, NR, T, T), BF16),
            pltpu.VMEM((2, 2, wide, wide), F32),
            pltpu.VMEM((2, 2, wide, wide), F32),
            pltpu.VMEM((2, 2, wide, wide), F32),
            pltpu.VMEM((2, 2, wide, wide), F32),
            pltpu.VMEM((2, 2, wide, wide), BF16),
            pltpu.VMEM((2, 2, wide, wide), BF16),
            pltpu.VMEM((NR, 2, T, T), F32),
            pltpu.VMEM((3, 2 * T, T), F32),
            pltpu.VMEM((3, 2 * T, T), F32),
            pltpu.VMEM((2, 4, T, T), F32),
            pltpu.VMEM((2, 4, 2, PIECES, T // 2 // PIECES, T), F32),
            pltpu.VMEM((2, HOPS, 2, PIECES, T // 2 // PIECES, T), F32),
            pltpu.VMEM((2, 2, 8, T), F32),
            pltpu.VMEM((Z, 8, T), F32),
            dma((4,)),
            dma((2, 2, 4)), dma((2, 2, 4)),
            dma((2, 4, NR, 4)), dma((2, 4, NR, 4)),
            dma((2, 4, NR)), dma((2, 4, NR)),
            dma((2, HOPS, 2, PIECES)), dma((2, HOPS, 2, PIECES)),
            dma((2, HOPS, 2, PIECES)), dma((2, HOPS, 2, PIECES)),
            dma((Z - 1,)), dma((Z - 1,)),
            dma((3,)), dma((3,)),
        ],
        compiler_params=pltpu.CompilerParams(
            collective_id=0, has_side_effects=True, vmem_limit_bytes=60 * 1024 * 1024
        ),
    )(pole_weight, face_tiles, root_factor[0], leaf_factor[0], leaf_upper[0], leaf_lower[0])
    return root[0, :band], leaf, face


def solution(mesh):
    return jax.shard_map(
        per_device,
        mesh=mesh,
        in_specs=(
            P("pole", None),
            P("pole", None, "snode", None),
            P("pole", "snode", None, None, None),
            P("pole", "snode", None, None, None),
            P("pole", "snode", None, None, None),
            P("snode", None),
        ),
        out_specs=(P("snode"), P("snode", None), P("snode", None, None)),
        check_vma=False,
    )
```

```python
import functools

import jax
import jax.numpy as jnp
from jax import lax
from jax.experimental import pallas as pl
from jax.experimental.pallas import tpu as pltpu
from jax.sharding import PartitionSpec as P

NR = 4
X = 4
Y = 4
Z = 8
HOPS = Z // 2
PIECES = 2
F32 = jnp.float32
BF16 = jnp.bfloat16


def split(value):
    high = value.astype(BF16)
    return high, (value - high.astype(F32)).astype(BF16)


def product(left, right):
    def three(a, b):
        ah, al = (jnp.concatenate([item[n] for item in left], 1) for n in (a, a + 1))
        bh, bl = (jnp.concatenate([item[n] for item in right], 0) for n in (b, b + 1))
        return jnp.dot(
            jnp.concatenate([ah, ah, al], 1), jnp.concatenate([bh, bl, bh], 0), preferred_element_type=F32
        )

    return jnp.concatenate([three(0, 0) - three(2, 2), three(0, 2) + three(2, 0)], 0)


def fold_rows(value):
    rows, cols = value.shape
    return jnp.sum(value.reshape(rows // 8, 8, cols), axis=0)


def kernel(
    T,
    w_ref, faces_ref, root_hbm, lf_hbm, lu_hbm, ll_hbm,
    face_out, leaf_out, root_out,
    root_all, fh, fl, gh, gl, lf, lu, lut, ll, lh, lo, pivots, given, taken, band_given, band_taken, imags, contrib, rs_buf, leaf_acc, small,
    in_sem, p1_s, p1_r, p2_s, p2_r, sib_s, sib_r, rs_s, rs_r, ag_s, ag_r, sm_s, sm_r, ex_s, ex_r,
):
    z = lax.axis_index("pole")
    s = lax.axis_index("snode")
    core = s % 2
    x = (s // 2) % X
    y = s // (2 * X)
    band = root_hbm.shape[1]
    half = band // 2
    sub = T // 2 // PIECES

    def at_xy(yy, xx, cc):
        return {"snode": (yy * X + xx) * 2 + cc}

    turn = 1 - 2 * core
    xp, xm, x2 = (x + turn + X) % X, (x - turn + X) % X, (x + 2) % X
    yp, ym, y2 = (y + turn + Y) % Y, (y - turn + Y) % Y, (y + 2) % Y
    zp, zm = (z + turn + Z) % Z, (z - turn + Z) % Z
    east, west = at_xy(y, xp, core), at_xy(y, xm, core)
    north, south = at_xy(yp, x, core), at_xy(ym, x, core)
    mate = at_xy(y, x, 1 - core)
    above, below = {"pole": zp}, {"pole": zm}

    def remote(src, dst, send, recv, to):
        return pltpu.make_async_remote_copy(
            src_ref=src, dst_ref=dst, send_sem=send, recv_sem=recv,
            device_id=to, device_id_type=pl.DeviceIdType.MESH,
        )

    sent = []

    def push(src, dst, send, recv, to):
        copy = remote(src, dst, send, recv, to)
        copy.start()
        sent.append(copy)

    def drain():
        for copy in sent:
            copy.wait_send()
        sent.clear()

    def arrived(dst, send, recv, to):
        remote(dst, dst, send, recv, to).wait_recv()

    barrier = pltpu.get_barrier_semaphore()
    for to in (east, west, north, south, mate, above, below):
        pl.semaphore_signal(barrier, inc=1, device_id=to, device_id_type=pl.DeviceIdType.MESH)

    loads = [
        pltpu.make_async_copy(root_hbm, root_all.at[:, y, x, core], in_sem.at[0]),
        pltpu.make_async_copy(lf_hbm, lf, in_sem.at[1]),
        pltpu.make_async_copy(lu_hbm, lu, in_sem.at[2]),
        pltpu.make_async_copy(ll_hbm, ll, in_sem.at[3]),
    ]
    for load in loads:
        load.start()
    pl.semaphore_wait(barrier, 7)

    everything = slice(None)
    fore, rear = pl.ds(0, half), pl.ds(half, half)
    halves = (pl.ds(2 * T, 2 * T), pl.ds(0, 2 * T))
    tiles = [pl.ds(wave * T, T) for wave in range(NR)]
    along = ((y, ym, yp, y2), (x, xm, xp, x2))
    across = ((x, xm, xp, x2), (y, ym, yp, y2))
    first_ways = ((east, west), (north, south))
    second_ways = ((north, south), (east, west))

    def spot(part, line, cross, rows, cols, other=core):
        if part == 0:
            return root_all.at[0, line, cross, other, rows, cols]
        return root_all.at[1, cross, line, other, rows, cols]

    def line_send(part, h):
        for number, to in enumerate(first_ways[part]):
            push(spot(part, along[part][0], across[part][0], everything, halves[h]),
                 spot(part, along[part][0], across[part][0], everything, halves[h]),
                 p1_s.at[part, h, number], p1_r.at[part, h, number], to)

    def line_near(part, h):
        for number, to in enumerate(first_ways[part]):
            cross = across[part][1 + number]
            arrived(spot(part, along[part][0], cross, everything, halves[h]),
                    p1_s.at[part, h, number], p1_r.at[part, h, number], to)
            piece = spot(part, along[part][0], cross, (fore, rear)[number], halves[h])
            push(piece, piece, p1_s.at[part, h, 2 + number], p1_r.at[part, h, 2 + number], to)

    def line_far(part, h):
        for number, to in enumerate(first_ways[part]):
            arrived(spot(part, along[part][0], across[part][3], (fore, rear)[number], halves[h]),
                    p1_s.at[part, h, 2 + number], p1_r.at[part, h, 2 + number], to)

    def near_send(part, group, cut):
        cols = (halves if group == 0 else tiles)[cut]
        for number, to in enumerate(second_ways[part]):
            piece = spot(part, along[part][0], across[part][group], everything, cols)
            push(piece, piece, p2_s.at[part, group, cut, number], p2_r.at[part, group, cut, number], to)

    def far_rows(group, number):
        if group in (0, 3):
            return (fore, rear)[number]
        return everything if group == 1 + number else None

    def near_in(part, group, cut):
        cols = (halves if group == 0 else tiles)[cut]
        for number, to in enumerate(second_ways[part]):
            line = along[part][1 + number]
            arrived(spot(part, line, across[part][group], everything, cols),
                    p2_s.at[part, group, cut, number], p2_r.at[part, group, cut, number], to)
            rows = far_rows(group, number)
            if rows is not None:
                piece = spot(part, line, across[part][group], rows, cols)
                push(piece, piece, p2_s.at[part, group, cut, 2 + number],
                     p2_r.at[part, group, cut, 2 + number], to)

    def far_in(part, group, cut):
        cols = (halves if group == 0 else tiles)[cut]
        for number, to in enumerate(second_ways[part]):
            rows = far_rows(group, number)
            if rows is not None:
                arrived(spot(part, along[part][3], across[part][group], rows, cols),
                        p2_s.at[part, group, cut, 2 + number], p2_r.at[part, group, cut, 2 + number], to)

    parts = (0, 1)

    def mate_lines(cut, numbers, cols, other):
        for part in parts:
            for number in numbers:
                yield part, number, spot(part, along[part][number], everything, everything, cols, other)

    def to_mate(cut, numbers, cols):
        for part, number, piece in mate_lines(cut, numbers, cols, core):
            push(piece, piece, sib_s.at[part, number, cut], sib_r.at[part, number, cut], mate)

    def from_mate(cut, numbers, cols):
        for part, number, piece in mate_lines(cut, numbers, cols, 1 - core):
            arrived(piece, sib_s.at[part, number, cut], sib_r.at[part, number, cut], mate)

    def relay_near(wave):
        for group in (1, 2, 3):
            for part in parts:
                near_in(part, group, wave)
        to_mate(wave, (1, 2), tiles[wave])

    def relay_far(wave):
        for group in (1, 2, 3):
            for part in parts:
                far_in(part, group, wave)
        to_mate(wave, (3,), tiles[wave])

    def waves_send(wave, groups):
        for group in groups:
            for part in parts:
                near_send(part, group, wave)

    def own_part(action, h):
        for part in parts:
            action(part, 0, h)

    def line_part(action, h):
        for part in parts:
            action(part, h)

    def own_line(h):
        to_mate(h, (0,), halves[h])

    def mate_line(h):
        from_mate(h, (0,), halves[h])

    loads[0].wait()
    line_part(line_send, 0)
    own_part(near_send, 0)

    wr = w_ref[0, 0]
    wi = w_ref[0, 1]
    own_col = 3 - core
    edge = T // 2
    eye = (
        lax.broadcasted_iota(jnp.int32, (edge, edge), 0) == lax.broadcasted_iota(jnp.int32, (edge, edge), 1)
    )

    def weighted_diagonal(real, imag):
        found = []
        for begin in (0, edge):
            block = (slice(begin, begin + edge),) * 2
            found.append(fold_rows(jnp.where(eye, wr * real[block] - wi * imag[block], 0.0)))
        return jnp.sum(jnp.concatenate(found, 1), axis=0, keepdims=True)

    first, second = pl.ds(0, T), pl.ds(T, T)

    def leaf_inverse(leaf):
        pr, pi = lf[leaf, 0, second, second], lf[leaf, 1, second, second]
        inner = product(
            [split(pr) + split(pi)],
            [split(lf[leaf, 0, second, first]) + split(lf[leaf, 1, second, first])],
        )
        ur, ui = lf[leaf, 0, first, second].T, lf[leaf, 1, first, second].T
        tr, ti = inner[:T], inner[T:]
        total = ur * (wr * tr - wi * ti) - ui * (wr * ti + wi * tr)
        base = weighted_diagonal(lf[leaf, 0, first, first], lf[leaf, 1, first, first])
        rows = lax.broadcasted_iota(jnp.int32, (8, T), 0) == 0
        leaf_acc[leaf, 0] = fold_rows(total) + jnp.where(rows, base, 0.0)
        leaf_acc[leaf, 1] = jnp.where(rows, weighted_diagonal(pr, pi), 0.0)

    def turn_upper(leaf):
        for part in range(2):
            for row in (first, second):
                for col in (first, second):
                    lut[leaf, part, col, row] = lu[leaf, part, row, col].T

    def split_lower(leaf):
        for part in range(2):
            for row in (first, second):
                lh[leaf, part, row], lo[leaf, part, row] = split(ll[leaf, part, row])

    def load_wave(wave):
        for part in range(2):
            for row in range(NR):
                if row != wave:
                    tile = root_all[part, row, :, :, :, pl.ds(wave * T, T)].reshape(T, T)
                    fh[part, row, wave], fl[part, row, wave] = split(tile)

    def tile_of(high, lower, row, col):
        return high[0, row, col], lower[0, row, col], high[1, row, col], lower[1, row, col]

    def put(row, col, value):
        gh[0, row, col], gl[0, row, col] = split(value[:T])
        gh[1, row, col], gl[1, row, col] = split(value[T:])

    def upper_part(k, after, col):
        return product([tile_of(fh, fl, k, m) for m in after], [tile_of(gh, gl, m, col) for m in after])

    def uppers(k, cols):
        for col in cols:
            put(k, col, -upper_part(k, range(k + 1, NR), col))

    def hand(number):
        push(given.at[number], taken.at[number], ex_s.at[number], ex_r.at[number], mate)

    def receive(number, row, col):
        arrived(taken.at[number], ex_s.at[number], ex_r.at[number], mate)
        put(row, col, taken[number])

    def own_upper_one():
        value = -upper_part(1, (2, 3), own_col)
        put(1, own_col, value)
        given[0] = value
        hand(0)
        given[1] = upper_part(0, (2, 3), own_col)

    def own_upper_zero():
        value = -(given[1] + upper_part(0, (1,), own_col))
        put(0, own_col, value)
        given[1] = value
        hand(1)

    def put_band(owner, value):
        rows = pl.ds(pl.multiple_of(owner * (T // 2), T // 2), T // 2)
        gh[0, 0, 1, rows], gl[0, 0, 1, rows] = split(value[: T // 2])
        gh[1, 0, 1, rows], gl[1, 0, 1, rows] = split(value[T // 2 :])

    def own_band_one():
        after = (1, 2, 3)
        rows = pl.ds(pl.multiple_of(core * (T // 2), T // 2), T // 2)
        left = [(fh[0, 0, m, rows], fl[0, 0, m, rows], fh[1, 0, m, rows], fl[1, 0, m, rows]) for m in after]
        value = -product(left, [tile_of(gh, gl, m, 1) for m in after])
        put_band(core, value)
        band_given[...] = value
        push(band_given, band_taken, ex_s.at[3], ex_r.at[3], mate)

    def receive_band():
        arrived(band_taken, ex_s.at[3], ex_r.at[3], mate)
        put_band(1 - core, band_taken[...])

    def own_lower_zero():
        row, after = 3 - core, (1, 2, 3)
        value = -product([tile_of(gh, gl, row, m) for m in after], [tile_of(fh, fl, m, 0) for m in after])
        put(row, 0, value)
        given[2] = value
        hand(2)

    def lowers(rows, k):
        after = range(k + 1, NR)
        for row in rows:
            put(row, k, -product([tile_of(gh, gl, row, m) for m in after], [tile_of(fh, fl, m, k) for m in after]))

    def pivot(k):
        cols = pl.ds(k * T, T)
        real = root_all[0, k, :, :, :, cols].reshape(T, T)
        imag = root_all[1, k, :, :, :, cols].reshape(T, T)
        after = range(k + 1, NR)
        if after:
            lost = product([tile_of(fh, fl, k, m) for m in after], [tile_of(gh, gl, m, k) for m in after])
            real = real - lost[:T]
            imag = imag - lost[T:]
        gh[0, k, k], gl[0, k, k] = split(real)
        gh[1, k, k], gl[1, k, k] = split(imag)
        pivots[k, 0] = real
        pivots[k, 1] = imag

    def root_diagonal(k):
        small[z, 4 + k : 5 + k] = weighted_diagonal(pivots[k, 0], pivots[k, 1])

    loads[1].wait()
    leaf_inverse(0)
    line_part(line_near, 0)
    waves_send(3, (1, 2))
    line_part(line_send, 1)
    waves_send(2, (1, 2))
    leaf_inverse(1)
    line_part(line_far, 0)
    waves_send(3, (3,))
    waves_send(2, (3,))
    own_line(0)
    own_part(near_send, 1)
    own_part(near_in, 0)
    line_part(line_near, 1)
    loads[3].wait()
    split_lower(0)
    relay_near(3)
    split_lower(1)
    line_part(line_far, 1)
    own_line(1)
    waves_send(1, (1, 2, 3))
    loads[2].wait()
    turn_upper(0)
    relay_near(2)
    own_part(far_in, 0)
    relay_far(3)
    own_part(near_in, 1)
    waves_send(0, (1, 2, 3))
    turn_upper(1)
    mate_line(0)
    from_mate(3, (1, 2, 3), tiles[3])
    load_wave(3)
    pivot(3)
    uppers(2, (3,))
    relay_near(1)
    relay_far(2)
    from_mate(2, (1, 2, 3), tiles[2])
    load_wave(2)
    lowers((3,), 2)
    pivot(2)
    relay_near(0)
    own_part(far_in, 1)
    relay_far(1)
    own_upper_one()
    mate_line(1)
    from_mate(1, (1, 2, 3), tiles[1])
    load_wave(1)
    lowers((3, 2), 1)
    relay_far(0)
    pivot(1)
    own_upper_zero()
    own_band_one()
    receive(0, 1, 2 + core)
    receive(1, 0, 2 + core)
    from_mate(0, (1, 2, 3), tiles[0])
    load_wave(0)
    own_lower_zero()
    lowers((1,), 0)
    receive_band()
    receive(2, 2 + core, 0)
    pivot(0)

    def quarter(leaf, number):
        qr, qc = number // 2, number % 2
        cols = pl.ds(pl.multiple_of(qc * T, T), T)
        row = faces_ref[leaf, qr]
        lefts, rights = [], []
        for face in range(2):
            col = faces_ref[leaf, face]
            lefts.append(tile_of(gh, gl, row, col))
            inner = pl.ds(face * T, T)
            rights.append((lh[leaf, 0, inner, cols], lo[leaf, 0, inner, cols],
                           lh[leaf, 1, inner, cols], lo[leaf, 1, inner, cols]))
        block = -product(lefts, rights)
        real, imag = block[:T], block[T:]
        dr = wr * real - wi * imag
        di = wr * imag + wi * real
        contrib[leaf, number] = dr.reshape(2, PIECES, sub, T)
        imags[leaf, number] = di

    def leaf_diagonal(leaf, number):
        qr, qc = number // 2, number % 2
        rows, cols = pl.ds(qr * T, T), pl.ds(qc * T, T)
        dr = contrib[leaf, number].reshape(T, T)
        lost = lut[leaf, 0, rows, cols] * dr - lut[leaf, 1, rows, cols] * imags[leaf, number]
        leaf_acc[leaf, qc] = leaf_acc[leaf, qc] - fold_rows(lost)

    onward = (above, below)
    turns = (turn, -turn)
    lean = 2 * (z % 2) - 1

    def quarter_step(leaf, step):
        shift = (0, lean, -lean, 2)[step]
        quarter(leaf, ((z + 4) // 2 + shift + 8) % 4)

    def mine(leaf, number, piece):
        return contrib.at[leaf, number // 2, number % 2, piece]

    def place(leaf, number, piece):
        block, part = number // 2, number % 2
        row = pl.multiple_of((block // 2) * T + part * (T // 2) + piece * sub, sub)
        col = pl.multiple_of((block % 2) * T, T)
        return face_out.at[leaf, pl.ds(row, sub), pl.ds(col, T)]

    def owner(way, step):
        return (z + turns[way] * (HOPS - step) + Z) % Z

    def scatter_send(way, step, leaf, piece, src):
        push(src, rs_buf.at[way, step, leaf, piece], rs_s.at[way, step, leaf, piece],
             rs_r.at[way, step, leaf, piece], onward[way])

    def scatter_wait(way, step, leaf, piece):
        slot = rs_buf.at[way, step, leaf, piece]
        arrived(slot, rs_s.at[way, step, leaf, piece], rs_r.at[way, step, leaf, piece], onward[way])
        return slot

    def scatter_first(way, step, leaf):
        for piece in range(PIECES):
            scatter_send(way, step, leaf, piece, mine(leaf, owner(way, step), piece))

    def scatter_on(step, leaf, piece, way):
        slot = scatter_wait(way, step - 1, leaf, piece)
        slot[...] = slot[...] + mine(leaf, owner(way, step), piece)[...]
        scatter_send(way, step, leaf, piece, slot)

    def gather_send(way, step, leaf, piece):
        where = place(leaf, (z - turns[way] * step + Z) % Z, piece)
        push(where, where, ag_s.at[way, step, leaf, piece], ag_r.at[way, step, leaf, piece], onward[way])

    def gather_on(step, leaf, piece, way):
        where = place(leaf, (z - turns[way] * (step + 1) + Z) % Z, piece)
        arrived(where, ag_s.at[way, step, leaf, piece], ag_r.at[way, step, leaf, piece], onward[way])
        if step + 1 < HOPS - 1 or (step + 1 < HOPS and way == leaf):
            gather_send(way, step + 1, leaf, piece)

    earlier = sent[:]
    sent.clear()
    for leaf in range(2):
        quarter_step(leaf, 0)
        scatter_first(leaf, 0, leaf)
    for leaf in range(2):
        quarter_step(leaf, 1)
        scatter_first(1 - leaf, 1, leaf)
    for copy in earlier:
        copy.wait_send()
    for leaf in range(2):
        for piece in range(PIECES):
            scatter_on(1, leaf, piece, leaf)
    for step in range(2, HOPS):
        for leaf in range(2):
            quarter_step(leaf, step)
            for piece in range(PIECES):
                for way in range(2):
                    scatter_on(step, leaf, piece, way)

    def small_send(step):
        where = small.at[(z - turn * step + Z) % Z]
        push(where, where, sm_s.at[step], sm_r.at[step], above)

    def small_on(step):
        arrived(small.at[(z - turn * (step + 1) + Z) % Z], sm_s.at[step], sm_r.at[step], above)
        if step < Z - 2:
            small_send(step + 1)

    for leaf in range(2):
        for piece in range(PIECES):
            up = scatter_wait(0, HOPS - 1, leaf, piece)
            down = scatter_wait(1, HOPS - 1, leaf, piece)
            place(leaf, z, piece)[...] = up[...] + down[...] + mine(leaf, z, piece)[...]
            for way in range(2):
                gather_send(way, 0, leaf, piece)
    scattered = sent[:]
    sent.clear()
    for leaf in range(2):
        for number in range(4):
            leaf_diagonal(leaf, number)
    for leaf in range(2):
        for col in range(2):
            row = 2 * leaf + col
            small[z, row : row + 1] = jnp.sum(leaf_acc[leaf, col], axis=0, keepdims=True)
    for k in range(NR):
        root_diagonal(k)
    small_send(0)
    for step in range(HOPS):
        if step == 2:
            for copy in scattered:
                copy.wait_send()
        for leaf in range(2):
            for piece in range(PIECES):
                for way in range(2):
                    if step < HOPS - 1 or way == leaf:
                        gather_on(step, leaf, piece, way)
            if 2 * step + leaf < Z - 1:
                small_on(2 * step + leaf)
    total = jnp.sum(small[...], axis=0)
    for leaf in range(2):
        for col in range(2):
            row = 2 * leaf + col
            leaf_out[leaf : leaf + 1, col * T : (col + 1) * T] = total[row : row + 1]
    root_row = jnp.zeros((1, T), F32)
    for k in range(NR):
        root_row = root_row + jnp.where(y == k, total[4 + k : 5 + k], 0.0)
    root_row = pltpu.roll(root_row, (T - (x * 2 + core) * band) % T, 1)
    root_out[...] = root_row[:, :128]
    drain()


def per_device(pole_weight, root_factor, leaf_factor, leaf_upper, leaf_lower, face_tiles):
    T = root_factor.shape[-1] // NR
    band = root_factor.shape[2]
    wide = 2 * T
    whole = pl.BlockSpec(memory_space=pl.ANY)
    scalars = pl.BlockSpec(memory_space=pltpu.SMEM)
    vmem = pl.BlockSpec(memory_space=pltpu.VMEM)
    dma = pltpu.SemaphoreType.DMA
    face, leaf, root = pl.pallas_call(
        functools.partial(kernel, T),
        out_shape=(
            pltpu.VMEM((2, wide, wide), F32),
            pltpu.VMEM((2, wide), F32),
            pltpu.VMEM((1, 128), F32),
        ),
        in_specs=[scalars, scalars, whole, whole, whole, whole],
        out_specs=(vmem, vmem, vmem),
        scratch_shapes=[
            pltpu.VMEM((2, Y, X, 2, band, NR * T), F32),
            pltpu.VMEM((2, NR, NR, T, T), BF16),
            pltpu.VMEM((2, NR, NR, T, T), BF16),
            pltpu.VMEM((2, NR, NR, T, T), BF16),
            pltpu.VMEM((2, NR, NR, T, T), BF16),
            pltpu.VMEM((2, 2, wide, wide), F32),
            pltpu.VMEM((2, 2, wide, wide), F32),
            pltpu.VMEM((2, 2, wide, wide), F32),
            pltpu.VMEM((2, 2, wide, wide), F32),
            pltpu.VMEM((2, 2, wide, wide), BF16),
            pltpu.VMEM((2, 2, wide, wide), BF16),
            pltpu.VMEM((NR, 2, T, T), F32),
            pltpu.VMEM((3, 2 * T, T), F32),
            pltpu.VMEM((3, 2 * T, T), F32),
            pltpu.VMEM((T, T), F32),
            pltpu.VMEM((T, T), F32),
            pltpu.VMEM((2, 4, T, T), F32),
            pltpu.VMEM((2, 4, 2, PIECES, T // 2 // PIECES, T), F32),
            pltpu.VMEM((2, HOPS, 2, PIECES, T // 2 // PIECES, T), F32),
            pltpu.VMEM((2, 2, 8, T), F32),
            pltpu.VMEM((Z, 8, T), F32),
            dma((4,)),
            dma((2, 2, 4)), dma((2, 2, 4)),
            dma((2, 4, NR, 4)), dma((2, 4, NR, 4)),
            dma((2, 4, NR)), dma((2, 4, NR)),
            dma((2, HOPS, 2, PIECES)), dma((2, HOPS, 2, PIECES)),
            dma((2, HOPS, 2, PIECES)), dma((2, HOPS, 2, PIECES)),
            dma((Z - 1,)), dma((Z - 1,)),
            dma((4,)), dma((4,)),
        ],
        compiler_params=pltpu.CompilerParams(
            collective_id=0, has_side_effects=True, vmem_limit_bytes=60 * 1024 * 1024
        ),
    )(pole_weight, face_tiles, root_factor[0], leaf_factor[0], leaf_upper[0], leaf_lower[0])
    return root[0, :band], leaf, face


def solution(mesh):
    return jax.shard_map(
        per_device,
        mesh=mesh,
        in_specs=(
            P("pole", None),
            P("pole", None, "snode", None),
            P("pole", "snode", None, None, None),
            P("pole", "snode", None, None, None),
            P("pole", "snode", None, None, None),
            P("snode", None),
        ),
        out_specs=(P("snode"), P("snode", None), P("snode", None, None)),
        check_vma=False,
    )
```
